32 devices in a mesh: groups: 2 (over x), dp: 16 (over z, y, core).
Axes of the slice: x: 2, y: 2, z: 4, core: 2. Of those that a mesh axis runs over, the one named last changes fastest.
Arguments:
- features: bfloat16 [4096, 6144], P(('groups', 'dp')), parts along dimension 0, may hold values from -6 to 6
- grads: bfloat16 [4096, 16384], P(('groups', 'dp')), parts along dimension 0, may hold values from -6 to 6
- routes: int32 [4096, 2], P(('groups', 'dp')), parts along dimension 0, may hold values from 0 to 7, all different within a row; in each aligned block of 128 rows (0 to 127, 128 to 255, ...) at most 48 rows name the same one
- proj_in: bfloat16 [64, 49152], P(None, 'dp'), may hold values from -0.078125 to 0.078125
- proj_out: bfloat16 [64, 131072], P(None, 'dp'), may hold values from -0.046875 to 0.046875
- fisher_inverse: bfloat16 [4096, 4096], P(None, 'dp'), as said below
Outputs:
- preconditioned: float32 [32, 8, 4096], P(('groups', 'dp')), parts along dimension 0
The draws below stay inside these ranges and needn't reach their ends.
There are 2 independent parts, one for each index of `groups`. The reference program is written for one: setup_inputs(seed, part) draws one part's arguments, and reference() takes and returns one part's arrays. A program takes and returns all parts, laid end to end along the dimension named above; an argument that names none is the same for every part. Nothing has to cross between parts.
Inputs may be any that keep to these rules, and one draw needn't show every extreme that they name: `routes`: the two experts of a token differ; among the 128 rows of one device no expert is named more than 48 times, and in every draw some expert is named exactly 48 times by the rows of some device. `fisher_inverse`: the matrix is symmetric.
All inputs are finite; a program needn't handle non-finite values.
Results may differ from the reference program's by a relative error of at most 0.0029.
Values may be sent and summed in bfloat16 or wider, within the bound.
No kernel may reach another device: no remote copies, remote signals or barrier semaphores. Data moves between devices by JAX's collectives and lax.ppermute only.
A program may use at most 128 MiB of HBM per device.

```python
import math
import jax
import jax.numpy as jnp
import numpy as np
from jax import lax

D = 6144
FF = 16384
EXPERTS = 8
TOP = 2
PROJ = 64
TOK_EX = 128
TOK_DEV = 128
CAP = 48
PD = 4096
TOKENS = 2048
N_DP = 16


def draw_fisher_inverse(key, part):
    key = jax.random.fold_in(key, 7)
    noise = jax.random.truncated_normal(key, -4.0, 4.0, (PD, PD), jnp.float32)
    symmetric = (noise + noise.T) * (0.35 / (2.0 * PD) ** 0.5)
    rows = jnp.arange(PD, dtype=jnp.int32)
    identity = (rows[:, None] == rows[None, :]).astype(jnp.float32)
    return (identity + symmetric).astype(jnp.bfloat16)


def block_levels(key, shape, pieces, low, high):
    level = 1.0
    for position, blocks in pieces:
        steps = jax.random.uniform(jax.random.fold_in(jax.random.fold_in(key, 6), position), (blocks,), jnp.float32, low / len(pieces), high / len(pieces))
        level = level * jnp.repeat(jnp.exp(steps), shape[position] // blocks).reshape((-1,) + (1,) * (len(shape) - 1 - position))
    return level


def deal_out(rng, own, number, rows, number_of, top, bound, lean):
    sequence = jax.random.permutation(rng, number_of)
    packed, common = portions_of(number_of, rows * top, bound, lean, True), portions_of(number_of, rows * top, bound, lean, False)
    places = jnp.arange(number_of)

    def named(lengths, offset_by):
        used = int((lengths > 0).sum())
        fixed = max(1, used // 4)
        moved = fixed + (places - fixed + offset_by * (used - fixed)) % max(1, number_of - fixed)
        return jnp.zeros((number_of,), jnp.int32).at[sequence[jnp.where(places < fixed, places, moved)]].set(jnp.asarray(lengths, jnp.int32))

    lengths = jnp.where(number % 4 == 0, named(packed, number // 4), named(common, number - number // 4 - 1))
    mixed = jax.random.permutation(jax.random.fold_in(own, 3), number_of)
    giver, taker = mixed[0:number_of // 2 * 2:2], mixed[1:number_of // 2 * 2:2]
    margin = jnp.minimum(lengths[giver] - 1, bound - lengths[taker]) // 2
    margin = jnp.where((giver == sequence[0]) | (taker == sequence[0]) | (lengths[taker] == 0), 0, jnp.maximum(margin, 0))
    moved = jax.random.randint(jax.random.fold_in(own, 4), (number_of // 2,), 0, 1 << 20) % (margin + 1)
    lengths = lengths.at[giver].add(-moved).at[taker].add(moved)
    labels = jnp.searchsorted(jnp.cumsum(lengths), jnp.arange(rows * top), side="right").astype(jnp.int32)
    table = labels.reshape(top, rows).T
    table = table[jax.random.permutation(jax.random.fold_in(own, 1), rows)]
    offset_by = jax.random.randint(jax.random.fold_in(own, 2), (rows, 1), 0, top)
    return jnp.take_along_axis(table, (jnp.arange(top)[None, :] + offset_by) % top, axis=1)


def portions_of(count, total, most, slope, full):
    weights = [(1 << 20) // math.isqrt(standing ** slope) + 1 for standing in range(1, count + 1)]
    largest = most if full else min(most, max(-(-total // count), total * weights[0] // sum(weights)))
    least = 1 if total - largest >= count - 1 else 0
    counts, spare = [largest] + [least] * (count - 1), total - largest - least * (count - 1)
    while spare > 0:
        free = [i for i in range(1, count) if counts[i] < largest] or [i for i in range(1, count) if counts[i] < most]
        pool, remaining = sum([weights[i] for i in free]), spare
        for i in free:
            addition = min(most - counts[i], max(1, remaining * weights[i] // pool), spare)
            counts[i] = counts[i] + addition
            spare = spare - addition
    return np.array(counts)


def bell_draw(own_key, shape, spread, bound, pieces=(), kind=jnp.bfloat16):
    values = jax.random.normal(own_key, shape, jnp.float32) * spread
    if len(pieces) > 0:
        values = block_levels(own_key, shape, pieces, -0.22, 0.18) * values
    return jnp.clip(values, min=-bound, max=bound).astype(kind)


def setup_inputs(seed: int = 0, part: int = 0) -> dict:
    streams_of = jax.random.split(jax.random.key(seed), 7)
    part_splits = jax.random.split(jax.random.fold_in(streams_of[6], part), 7)
    features = bell_draw(part_splits[0], (TOKENS, D), 1.0, 6.0, ((0, 16),))
    grads = bell_draw(part_splits[1], (TOKENS, FF), 1.0, 6.0, ((0, 16),))
    routes_keys = jax.random.split(jax.random.fold_in(part_splits[2], 1), TOKENS // TOK_DEV)
    routes_turns = jax.random.permutation(jax.random.fold_in(part_splits[2], 3), TOKENS // TOK_DEV)
    routes = jax.vmap(lambda own, number: deal_out(jax.random.fold_in(part_splits[2], 2), own, number, TOK_DEV, EXPERTS, TOP, CAP, 2))(routes_keys, routes_turns).reshape((TOKENS, TOP))
    proj_in = bell_draw(streams_of[3], (PROJ, EXPERTS * D), D ** -0.5, 0.078125, ((1, 16),))
    proj_out = bell_draw(streams_of[4], (PROJ, EXPERTS * FF), FF ** -0.5, 0.046875, ((1, 16),))
    fisher_inverse = draw_fisher_inverse(jax.random.fold_in(streams_of[6], 71), part)
    return dict(features=features, grads=grads, routes=routes, proj_in=proj_in, proj_out=proj_out, fisher_inverse=fisher_inverse)


def reference(features, grads, routes, proj_in, proj_out, fisher_inverse):
    tokens = features.shape[0]
    examples = tokens // TOK_EX
    limit = N_DP * CAP
    weights_in = proj_in.astype(jnp.float32).reshape(PROJ, EXPERTS, D)
    weights_out = proj_out.astype(jnp.float32).reshape(PROJ, EXPERTS, FF)

    def one_expert(expert):
        chosen = jnp.any(routes == expert, axis=1)
        order = jnp.argsort(jnp.where(chosen, 0, 1).astype(jnp.int32), stable=True)[:limit]
        valid = chosen[order].astype(jnp.float32)
        rows_in = features[order].astype(jnp.float32)
        rows_out = grads[order].astype(jnp.float32)
        left = jnp.dot(rows_in, weights_in[:, expert, :].T, precision=lax.Precision.HIGHEST)
        right = jnp.dot(rows_out, weights_out[:, expert, :].T, precision=lax.Precision.HIGHEST)
        left = left * valid[:, None]
        member = ((order // TOK_EX)[None, :] == jnp.arange(examples, dtype=jnp.int32)[:, None]).astype(jnp.float32)
        member = member * valid[None, :]
        return jnp.einsum("sm,mp,mq->spq", member, left, right, precision=lax.Precision.HIGHEST)

    stacked = lax.map(one_expert, jnp.arange(EXPERTS, dtype=jnp.int32))
    grams = jnp.transpose(stacked, (1, 0, 2, 3)).reshape(examples * EXPERTS, PD)
    grams = (grams * (TOK_EX ** -0.5)).astype(jnp.bfloat16)
    result = jnp.dot(grams, fisher_inverse, preferred_element_type=jnp.float32)
    return result.reshape(examples, EXPERTS, PD)
```

```python
import math

import jax
import jax.numpy as jnp
from jax import lax
from jax.experimental import pallas as pl
from jax.experimental.pallas import tpu as pltpu
from jax.sharding import PartitionSpec as P

EXPERTS = 8
PROJ = 64
TOK = 128
LANES = 128
VMEM = 48 * 1024 * 1024
AXES = ("groups", "dp")


def project_kernel(n_pieces, sub, n_in, n_a, n_k, eid_ref, *refs):
    toks = refs[: 4 * sub]
    w_a = refs[4 * sub : 4 * sub + n_pieces]
    w_b = refs[4 * sub + n_pieces : 4 * sub + 2 * n_pieces]
    routes_ref, out_ref, left, right = refs[4 * sub + 2 * n_pieces :]
    step = pl.program_id(0)

    @pl.when(step == 0)
    def _():
        left[...] = jnp.zeros_like(left)
        right[...] = jnp.zeros_like(right)

    def add(weights, total):
        table = jnp.concatenate([w[...] for w in weights], axis=0)
        for a in range(sub):
            rows = jnp.concatenate([toks[a * 4 + b][...] for b in range(4)], axis=0)
            total[a] += lax.dot_general(
                rows, table, (((1,), (1,)), ((), ())), preferred_element_type=jnp.float32
            )

    @pl.when(step < n_in)
    def _():
        add(w_a, left)

    @pl.when((step >= n_in) & (step < n_a))
    def _():
        add(w_a, right)

    @pl.when(step >= n_a)
    def _():
        add(w_b, right)

    @pl.when(step == n_k - 1)
    def _():
        low = lax.broadcasted_iota(jnp.int32, (TOK, LANES), 1) < PROJ
        for b in range(4):
            for k in range(2):
                own = routes_ref[b * TOK : (b + 1) * TOK, k : k + 1]
                picked = [jnp.zeros((TOK, LANES), jnp.float32) for _ in range(2)]
                for a in range(sub):
                    for pair in range(n_pieces // 2):
                        wanted = jnp.where(
                            low,
                            jnp.where(eid_ref[1, 2 * pair] == a, eid_ref[0, 2 * pair], -1),
                            jnp.where(eid_ref[1, 2 * pair + 1] == a, eid_ref[0, 2 * pair + 1], -1),
                        )
                        mask = own == wanted
                        for side, total in enumerate((left, right)):
                            block = total[a, b * TOK : (b + 1) * TOK, pair * LANES : (pair + 1) * LANES]
                            picked[side] += jnp.where(mask, block, 0.0)
                both = [x + pltpu.roll(x, PROJ, 1) for x in picked]
                out_ref[b, :, k * LANES : (k + 1) * LANES] = jnp.where(low, both[0], both[1])


def project(toks, pieces_a, pieces_b, routes, eid, sub, n_in, n_a, n_k, width):
    n_pieces = len(pieces_a)
    n_b = n_k - n_a

    def tok_spec(a):
        return pl.BlockSpec((TOK, width), lambda k, a=a: (0, a * n_k + k))

    specs = [pl.BlockSpec(memory_space=pltpu.SMEM)]
    operands = [eid]
    for a in range(sub):
        for tok in toks:
            specs.append(tok_spec(a))
            operands.append(tok)
    for piece in pieces_a:
        specs.append(pl.BlockSpec((PROJ, width), lambda k: (0, jnp.minimum(k, n_a - 1))))
        operands.append(piece)
    for piece in pieces_b:
        specs.append(pl.BlockSpec((PROJ, width), lambda k: (0, jnp.maximum(k - n_a, 0))))
        operands.append(piece)
    specs.append(pl.BlockSpec((4 * TOK, 2), lambda k: (0, 0)))
    operands.append(routes)
    total = pltpu.VMEM((sub, 4 * TOK, n_pieces * PROJ), jnp.float32)
    return pl.pallas_call(
        lambda *refs: project_kernel(n_pieces, sub, n_in, n_a, n_k, *refs),
        grid=(n_k,),
        in_specs=specs,
        out_specs=pl.BlockSpec((4, TOK, 4 * PROJ), lambda k: (0, 0, 0)),
        out_shape=jax.ShapeDtypeStruct((4, TOK, 4 * PROJ), jnp.float32),
        scratch_shapes=[total, total],
        compiler_params=pltpu.CompilerParams(vmem_limit_bytes=VMEM),
        name="project",
    )(*operands)


def gram_kernel(p0, p1, p2, p3, routes_ref, out_ref, flat):
    total = (p0[...] + p1[...]) + (p2[...] + p3[...])
    first, second = total[:, :LANES], total[:, LANES:]
    left = jnp.concatenate([jnp.transpose(first)[:PROJ], jnp.transpose(second)[:PROJ]], axis=1)
    right = jnp.concatenate([first, second], axis=0)
    named = routes_ref[...]
    rows = jnp.concatenate([jnp.where(named == e, left, 0.0) for e in range(EXPERTS)], axis=0)
    grams = lax.dot_general(
        rows,
        right,
        (((1,), (0,)), ((), ())),
        precision=lax.Precision.HIGHEST,
        preferred_element_type=jnp.float32,
    )
    grams = grams * (TOK**-0.5)
    low = lax.broadcasted_iota(jnp.int32, (PROJ // 2, LANES), 1) < PROJ
    for e in range(EXPERTS):
        top = grams[e * PROJ : e * PROJ + PROJ // 2]
        bottom = grams[e * PROJ + PROJ // 2 : (e + 1) * PROJ]
        flat[:, e, :] = jnp.where(low, pltpu.roll(top, PROJ, 1), bottom)
    out_ref[...] = flat[...].reshape(PROJ // 4, 2 * EXPERTS, LANES).astype(jnp.bfloat16)


def gram(parts, routes):
    return pl.pallas_call(
        gram_kernel,
        out_shape=jax.ShapeDtypeStruct((PROJ // 4, 2 * EXPERTS, LANES), jnp.bfloat16),
        scratch_shapes=[pltpu.VMEM((PROJ // 2, EXPERTS, LANES), jnp.float32)],
        name="gram",
    )(*parts, routes)


def fisher_kernel(n, order_ref, *refs):
    own, other = refs[: n // 2], refs[n // 2]
    fisher, out_ref = refs[n // 2 + 1 :]
    total = jnp.zeros((n * EXPERTS, fisher.shape[1]), jnp.float32)
    for i in range(PROJ // 4):
        tiles = [x[i] for x in own] + [other[j, i] for j in range(n // 2)]
        rows = jnp.concatenate([x.astype(jnp.float32).reshape(1, 2, EXPERTS, LANES) for x in tiles], axis=0)
        for h in range(2):
            p = 2 * i + h
            table = jnp.concatenate(
                [
                    fisher[p * PROJ : (p + 1) * PROJ, :],
                    fisher[(PROJ // 2 + p) * PROJ : (PROJ // 2 + p + 1) * PROJ, :],
                ],
                axis=0,
            )
            lhs = rows[:, h].reshape(n * EXPERTS, LANES).astype(jnp.bfloat16)
            total += jnp.dot(lhs, table, preferred_element_type=jnp.float32)
    for j in range(n):
        out_ref[order_ref[j]] = total[j * EXPERTS : (j + 1) * EXPERTS]


def precondition(own, other, fisher, order):
    n = 2 * len(own)
    vmem = pl.BlockSpec(memory_space=pltpu.VMEM)
    return pl.pallas_call(
        lambda *refs: fisher_kernel(n, *refs),
        in_specs=[pl.BlockSpec(memory_space=pltpu.SMEM)] + [vmem] * (n // 2 + 2),
        out_specs=vmem,
        out_shape=jax.ShapeDtypeStruct((n, EXPERTS, fisher.shape[1]), jnp.float32),
        compiler_params=pltpu.CompilerParams(vmem_limit_bytes=VMEM),
        name="precondition",
    )(order, *own, other, fisher)


def shards(features, grads, routes, proj_in, proj_out, fisher_inverse):
    groups, n = lax.axis_size("groups"), lax.axis_size("dp")
    chips = n // 2
    slices = n // EXPERTS
    sub = slices // 2
    y_size = 2 if groups == 2 else 1
    z_size = chips // y_size
    group, place = lax.axis_index("groups"), lax.axis_index("dp")
    core, chip, half = place % 2, place // 2, group % 2
    z, y = chip // y_size, chip % y_size

    def move(x, to):
        pairs = []
        for g in range(groups):
            for d in range(n):
                tg, td = to(g, d)
                pairs.append((g * n + d, tg * n + td))
        return lax.ppermute(x, AXES, pairs)

    def to_core(g, d):
        return g, d ^ 1

    def to_x(g, d):
        return g ^ 1, d

    def to_x_core(g, d):
        return g ^ 1, d ^ 1

    def to_y(g, d):
        return g, d ^ 2

    def to_z(g, d):
        return g, (d + 2 * y_size) % n

    quarter_in, quarter_out = proj_in.shape[1] // 2, proj_out.shape[1] // 2

    def token_columns(c, h):
        parts = []
        for a in range(sub):
            at = (a * 2 + c) * 2 + h
            parts.append(lax.dynamic_slice_in_dim(features, at * quarter_in, quarter_in, 1))
            parts.append(lax.dynamic_slice_in_dim(grads, at * quarter_out, quarter_out, 1))
        return jnp.concatenate(parts, axis=1)

    table = jnp.concatenate(
        [
            lax.dynamic_slice_in_dim(proj_in, half * quarter_in, quarter_in, 1),
            lax.dynamic_slice_in_dim(proj_out, half * quarter_out, quarter_out, 1),
        ],
        axis=1,
    )
    width = math.gcd(quarter_in, quarter_out)
    n_k = (quarter_in + quarter_out) // width
    n_in = quarter_in // width
    n_a = max(n_in, (n_k + 1) // 2)
    first = [table[:, : n_a * width]]
    second = [table[:, n_a * width :]]

    tok_x = move(token_columns(core, 1 - half), to_x)
    tok_x_core = move(token_columns(1 - core, 1 - half), to_x_core)
    for _ in range(z_size - 1):
        first.append(move(first[-1], to_z))
        second.append(move(second[-1], to_z))
    chip_ids = [((z - k) % z_size) * y_size + y for k in range(z_size)]
    if y_size == 2:
        for k in range(z_size):
            first.append(move(first[k], to_y))
            second.append(move(second[k], to_y))
            chip_ids.append(((z - k) % z_size) * y_size + (1 - y))
    tok_core = move(token_columns(1 - core, half), to_core)
    tok_own = token_columns(core, half)
    pair_routes = jnp.concatenate([routes, move(routes, to_core)], axis=0)
    all_routes = jnp.concatenate([pair_routes, move(pair_routes, to_x)], axis=0)
    chip_ids = jnp.stack(chip_ids).astype(jnp.int32)
    eid = jnp.stack([2 * chip_ids // slices, 2 * chip_ids % slices // 2])

    partial = project(
        [tok_own, tok_core, tok_x, tok_x_core], first, second, all_routes, eid, sub, n_in, n_a, n_k, width
    )
    sums = [partial[0], move(partial[1], to_core), move(partial[2], to_x), move(partial[3], to_x_core)]
    mine = gram(sums, routes.T.reshape(1, -1))

    own = [mine]
    for k in range(1, chips):
        own.append(move(mine, lambda g, d, k=k: (g, d ^ (2 * k))))
    other = move(jnp.stack(own), to_core)
    steps = jnp.arange(chips, dtype=jnp.int32)
    order = jnp.concatenate([(chip ^ steps) * 2 + core, (chip ^ steps) * 2 + (1 - core)])
    columns = precondition(own, other, fisher_inverse, order.astype(jnp.int32))
    result = lax.all_to_all(columns, "dp", split_axis=0, concat_axis=0, tiled=True)
    return jnp.transpose(result, (1, 0, 2)).reshape(1, EXPERTS, PROJ * PROJ)


def solution(mesh):
    in_specs = (
        P(AXES, None),
        P(AXES, None),
        P(AXES, None),
        P(None, "dp"),
        P(None, "dp"),
        P(None, "dp"),
    )
    out_specs = P(AXES, None, None)
    return jax.shard_map(shards, mesh=mesh, in_specs=in_specs, out_specs=out_specs, check_vma=False)
```

```python
import functools

import jax
import jax.numpy as jnp
from jax import lax
from jax.experimental import pallas as pl
from jax.experimental.pallas import tpu as pltpu
from jax.sharding import PartitionSpec as P

EXPERTS = 8
PROJ = 64
TOK = 128
LANES = 128
VMEM = 28 * 1024 * 1024
AXES = ("groups", "dp")


def nt(rows, table):
    return lax.dot_general(rows, table, (((1,), (1,)), ((), ())), preferred_element_type=jnp.float32)


def pick(total, routes, eid_ref, first, pieces, sub):
    low = lax.broadcasted_iota(jnp.int32, (TOK, LANES), 1) < PROJ
    out = []
    for k in range(2):
        picked = jnp.zeros((TOK, LANES), jnp.float32)
        for a in range(sub):
            for pair in range(pieces // 2):
                even, odd = first + 2 * pair, first + 2 * pair + 1
                wanted = jnp.where(
                    low,
                    jnp.where(eid_ref[1, even] == a, eid_ref[0, even], -1),
                    jnp.where(eid_ref[1, odd] == a, eid_ref[0, odd], -1),
                ).astype(jnp.float32)
                picked += jnp.where(routes[:, k : k + 1] == wanted, total(a, pair), 0.0)
        out.append(picked + pltpu.roll(picked, PROJ, 1))
    return out


def right_sums(sub, width, toks, pieces):
    table = jnp.concatenate([p[:, :width] for p in pieces], axis=0)
    return [nt(toks[:, a * width : (a + 1) * width], table) for a in range(sub)]


def left_sums(sub, width, toks, pieces):
    table = jnp.concatenate([p[:, width:] for p in pieces], axis=0)
    at, size = sub * width, table.shape[1]
    return [nt(toks[:, at + a * size : at + (a + 1) * size], table) for a in range(sub)]


def picks(rows, tables, width, first, eid_ref, sub):
    toks = jnp.concatenate(rows, axis=0)
    right, left = right_sums(sub, width, toks, tables), left_sums(sub, width, toks, tables)
    low = lax.broadcasted_iota(jnp.int32, (TOK, LANES), 1) < PROJ
    picked = []
    for b in range(len(rows)):
        here = slice(b * TOK, (b + 1) * TOK)
        named = toks[here, -LANES:].astype(jnp.float32)

        def pick_of(sums):
            return pick(
                lambda a, pair: sums[a][here, pair * LANES : (pair + 1) * LANES], named, eid_ref, first, len(tables), sub
            )

        picked.append([jnp.where(low, x, y) for x, y in zip(pick_of(left), pick_of(right))])
    return picked


def early_kernel(sub, width, eid_ref, own, other, x, *refs):
    rows = [own[...], other[...], x[...]]
    for b, slots in enumerate(picks(rows, refs[:-1], width, 0, eid_ref, sub)):
        for k, got in enumerate(slots):
            refs[-1][b, :, k * LANES : (k + 1) * LANES] = got


def last_kernel(sub, width, n_pieces, eid_ref, own, other, x, xc, *refs):
    pieces, early_ref, outs = refs[:n_pieces], refs[n_pieces], refs[n_pieces + 1 :]
    rows = [own[...], other[...], x[...]]
    for b, slots in enumerate(picks(rows, pieces[-2:], width, n_pieces - 2, eid_ref, sub)):
        for k, got in enumerate(slots):
            lanes = slice(k * LANES, (k + 1) * LANES)
            outs[b][:, lanes] = early_ref[b, :, lanes] + got
    for k, got in enumerate(picks([xc[...]], pieces, width, 0, eid_ref, sub)[0]):
        outs[3][:, k * LANES : (k + 1) * LANES] = got


def pack_kernel(outputs, place_ref, *refs):
    n_outs = sum(len(cuts) for _, cuts in outputs)
    n_blocks = sum(len(blocks) for blocks, _ in outputs)
    ins, outs = refs[:n_blocks], refs[n_blocks : n_blocks + n_outs]
    buffers, in_sems, out_sems = refs[n_blocks + n_outs : -2], refs[-2], refs[-1]
    copies, i = [], 0
    for (blocks, _), buffer in zip(outputs, buffers):
        at, group = 0, []
        for _, width, place, scale, offset in blocks:
            start = pl.multiple_of((place_ref[place] * scale + offset) * width, LANES)
            group.append(
                pltpu.make_async_copy(ins[i].at[:, pl.ds(start, width)], buffer.at[:, at : at + width], in_sems.at[i])
            )
            at, i = at + width, i + 1
        copies.append(group)
    for group in copies:
        for copy in group:
            copy.start()
    back, i = [], 0
    for (_, cuts), buffer, group in zip(outputs, buffers, copies):
        for copy in group:
            copy.wait()
        at = 0
        for width in cuts:
            copy = pltpu.make_async_copy(buffer.at[:, at : at + width], outs[i], out_sems.at[i])
            copy.start()
            back.append(copy)
            at, i = at + width, i + 1
    for copy in back:
        copy.wait()


def pack(places, outputs, name):
    blocks = [b for out, _ in outputs for b in out]
    shapes = [(out[0][0].shape[0], width) for out, cuts in outputs for width in cuts]
    hbm = pl.BlockSpec(memory_space=pl.ANY)
    plain = [([(None,) + b[1:] for b in out], cuts) for out, cuts in outputs]
    return pl.pallas_call(
        functools.partial(pack_kernel, plain),
        in_specs=[pl.BlockSpec(memory_space=pltpu.SMEM)] + [hbm] * len(blocks),
        out_specs=[hbm] * len(shapes),
        out_shape=[jax.ShapeDtypeStruct(x, jnp.bfloat16) for x in shapes],
        scratch_shapes=[pltpu.VMEM((out[0][0].shape[0], sum(cuts)), jnp.bfloat16) for out, cuts in outputs]
        + [pltpu.SemaphoreType.DMA((len(blocks),)), pltpu.SemaphoreType.DMA((len(shapes),))],
        compiler_params=pltpu.CompilerParams(vmem_limit_bytes=2 * VMEM),
        name=name,
    )(places, *[b[0] for b in blocks])


def local(kernel, name, out_shape, operands, smem=0):
    vmem = pl.BlockSpec(memory_space=pltpu.VMEM)
    return pl.pallas_call(
        kernel,
        in_specs=[pl.BlockSpec(memory_space=pltpu.SMEM)] * smem + [vmem] * (len(operands) - smem),
        out_specs=jax.tree.map(lambda _: vmem, out_shape),
        out_shape=out_shape,
        compiler_params=pltpu.CompilerParams(vmem_limit_bytes=VMEM),
        name=name,
    )(*operands)


def gram_kernel(p0, p1, p2, p3, routes_ref, out_ref, flat):
    total = (p0[...] + p1[...]) + (p2[...] + p3[...])
    first, second = total[:, :LANES], total[:, LANES:]
    left = jnp.concatenate([jnp.transpose(first)[:PROJ], jnp.transpose(second)[:PROJ]], axis=1)
    right = jnp.concatenate([first, second], axis=0)
    named = routes_ref[...]
    rows = jnp.concatenate([jnp.where(named == e, left, 0.0) for e in range(EXPERTS)], axis=0)
    grams = lax.dot_general(
        rows,
        right,
        (((1,), (0,)), ((), ())),
        precision=lax.Precision.HIGHEST,
        preferred_element_type=jnp.float32,
    )
    grams = grams * (TOK**-0.5)
    low = lax.broadcasted_iota(jnp.int32, (PROJ // 2, LANES), 1) < PROJ
    for e in range(EXPERTS):
        top = grams[e * PROJ : e * PROJ + PROJ // 2]
        bottom = grams[e * PROJ + PROJ // 2 : (e + 1) * PROJ]
        flat[:, e, :] = jnp.where(low, pltpu.roll(top, PROJ, 1), bottom)
    out_ref[...] = flat[...].reshape(PROJ // 4, 2 * EXPERTS, LANES).astype(jnp.bfloat16)


def gram(parts, routes):
    return pl.pallas_call(
        gram_kernel,
        out_shape=jax.ShapeDtypeStruct((PROJ // 4, 2 * EXPERTS, LANES), jnp.bfloat16),
        scratch_shapes=[pltpu.VMEM((PROJ // 2, EXPERTS, LANES), jnp.float32)],
        name="gram",
    )(*parts, routes)


def fisher_kernel(n, order_ref, *refs):
    own, other = refs[: n // 2], refs[n // 2]
    fisher, out_ref = refs[n // 2 + 1 :]
    total = jnp.zeros((n * EXPERTS, fisher.shape[1]), jnp.float32)
    for i in range(PROJ // 4):
        tiles = [x[i] for x in own] + [other[j, i] for j in range(n // 2)]
        rows = jnp.concatenate([x.astype(jnp.float32).reshape(1, 2, EXPERTS, LANES) for x in tiles], axis=0)
        for h in range(2):
            p = 2 * i + h
            table = jnp.concatenate(
                [
                    fisher[p * PROJ : (p + 1) * PROJ, :],
                    fisher[(PROJ // 2 + p) * PROJ : (PROJ // 2 + p + 1) * PROJ, :],
                ],
                axis=0,
            )
            lhs = rows[:, h].reshape(n * EXPERTS, LANES).astype(jnp.bfloat16)
            total += jnp.dot(lhs, table, preferred_element_type=jnp.float32)
    for j in range(n):
        out_ref[order_ref[j]] = total[j * EXPERTS : (j + 1) * EXPERTS]


def precondition(own, other, fisher, order):
    n = 2 * len(own)
    vmem = pl.BlockSpec(memory_space=pltpu.VMEM)
    return pl.pallas_call(
        lambda *refs: fisher_kernel(n, *refs),
        in_specs=[pl.BlockSpec(memory_space=pltpu.SMEM)] + [vmem] * (n // 2 + 2),
        out_specs=vmem,
        out_shape=jax.ShapeDtypeStruct((n, EXPERTS, fisher.shape[1]), jnp.float32),
        compiler_params=pltpu.CompilerParams(vmem_limit_bytes=VMEM),
        name="precondition",
    )(order, *own, other, fisher)


def shards(features, grads, routes, proj_in, proj_out, fisher_inverse):
    groups, n = lax.axis_size("groups"), lax.axis_size("dp")
    chips = n // 2
    slices = n // EXPERTS
    sub = slices // 2
    y_size = 2 if groups == 2 else 1
    z_size = chips // y_size
    group, place = lax.axis_index("groups"), lax.axis_index("dp")
    core, chip, half = place % 2, place // 2, group % 2
    z, y = chip // y_size, chip % y_size

    def move(x, to):
        pairs = []
        for g in range(groups):
            for d in range(n):
                tg, td = to(g, d)
                pairs.append((g * n + d, tg * n + td))
        return lax.ppermute(x, AXES, pairs)

    def to_core(g, d):
        return g, d ^ 1

    def to_x(g, d):
        return g ^ 1, d

    def to_x_core(g, d):
        return g ^ 1, d ^ 1

    def to_y(g, d):
        return g, d ^ 2

    def to_z(g, d):
        return g, (d + 2 * y_size) % n

    def from_z(g, d):
        return g, (d - 2 * y_size) % n

    quarter_in, quarter_out = proj_in.shape[1] // 2, proj_out.shape[1] // 2

    def after(x, *others):
        return lax.optimization_barrier((x, *others))[0]

    def part(c, h):
        return c * 2 + h

    places = jnp.stack([part(core, 1 - half), part(1 - core, 1 - half), part(core, half), part(1 - core, half), half])
    places = places.astype(jnp.int32)
    named = jnp.pad(routes.astype(jnp.bfloat16), ((0, 0), (0, LANES - 2)))
    width = sub * (quarter_in + quarter_out) + LANES

    def whole(place):
        return (
            [(grads, quarter_out, place, 1, 4 * a) for a in range(sub)]
            + [(features, quarter_in, place, 1, 4 * a) for a in range(sub)]
            + [(named, LANES, 0, 0, 0)]
        )

    tables = [(proj_out, quarter_out, 4, 1, 0), (proj_in, quarter_in, 4, 1, 0)]
    table, send_other, send_x = pack(
        places, [(tables, [quarter_out + quarter_in]), (whole(3), [width]), (whole(0), [width])], "pack_first"
    )
    send_xc, own = pack(after(places, send_x), [(whole(1), [width]), (whole(2), [width])], "pack_second")
    other = move(send_other, to_core)
    x, xc = move(send_x, to_x), move(send_xc, to_x_core)

    blocks, ids = [table], [0]
    ups, downs = z_size // 2, (z_size - 1) // 2
    up = down = table
    facing = move(table, to_y) if y_size == 2 else table
    for k in range(1, ups + 1):
        up = move(after(up, facing, other) if k == 2 else up, to_z)
        blocks.append(up)
        ids.append(-k)
        if k <= downs:
            down = move(down, from_z)
            blocks.append(down)
            ids.append(k)
    pieces, chip_ids = [], []
    for i, block in enumerate(blocks):
        for across in range(y_size):
            if across:
                if i == 1:
                    block = after(block, facing)
                if i == len(blocks) - 1:
                    block = after(block, x, pieces[3])
                block = move(block, to_y) if i else facing
            pieces.append(block)
            chip_ids.append(((z + ids[i]) % z_size) * y_size + (1 - y if across else y))

    chip_ids = jnp.stack(chip_ids).astype(jnp.int32)
    eid = jnp.stack([2 * chip_ids // slices, 2 * chip_ids % slices // 2])

    f32 = jnp.float32
    early = local(
        functools.partial(early_kernel, sub, quarter_out),
        "project_early",
        jax.ShapeDtypeStruct((3, TOK, 2 * LANES), f32),
        [eid, own, other, x] + pieces[:-2],
        smem=1,
    )
    partial = local(
        functools.partial(last_kernel, sub, quarter_out, chips),
        "project_last",
        [jax.ShapeDtypeStruct((TOK, 2 * LANES), f32)] * 4,
        [eid, own, other, x, xc] + pieces + [early],
        smem=1,
    )
    sums = [partial[0], move(partial[1], to_core), move(partial[2], to_x), move(partial[3], to_x_core)]
    mine = gram(sums, routes.T.reshape(1, -1))

    own = [mine]
    for k in range(1, chips):
        own.append(move(mine, lambda g, d, k=k: (g, d ^ (2 * k))))
    other = move(jnp.stack(own), to_core)
    steps = jnp.arange(chips, dtype=jnp.int32)
    order = jnp.concatenate([(chip ^ steps) * 2 + core, (chip ^ steps) * 2 + (1 - core)])
    columns = precondition(own, other, fisher_inverse, order.astype(jnp.int32))
    result = lax.all_to_all(columns, "dp", split_axis=0, concat_axis=0, tiled=True)
    return jnp.transpose(result, (1, 0, 2)).reshape(1, EXPERTS, PROJ * PROJ)


def solution(mesh):
    in_specs = (
        P(AXES, None),
        P(AXES, None),
        P(AXES, None),
        P(None, "dp"),
        P(None, "dp"),
        P(None, "dp"),
    )
    out_specs = P(AXES, None, None)
    return jax.shard_map(shards, mesh=mesh, in_specs=in_specs, out_specs=out_specs, check_vma=False)
```

```python
import functools

import jax
import jax.numpy as jnp
from jax import lax
from jax.experimental import pallas as pl
from jax.experimental.pallas import tpu as pltpu
from jax.sharding import PartitionSpec as P

EXPERTS = 8
PROJ = 64
TOK = 128
LANES = 128
VMEM = 28 * 1024 * 1024
AXES = ("groups", "dp")


def position():
    place = lax.axis_index("dp")
    return lax.rem(place, 2), lax.div(place, 2), lax.rem(lax.axis_index("groups"), 2)


def piece_of(at, sizes):
    z_size, y_size, slices = sizes
    _, chip, _ = position()
    z, y = lax.div(chip, y_size), lax.rem(chip, y_size)
    step, across = at
    first = 2 * (lax.rem(z + (step + z_size), z_size) * y_size + (1 - y if across else y))
    return lax.div(first, slices), lax.div(lax.rem(first, slices), 2)


def nt(rows, table):
    return lax.dot_general(rows, table, (((1,), (1,)), ((), ())), preferred_element_type=jnp.float32)


def pick(total, routes, experts, sub):
    low = lax.broadcasted_iota(jnp.int32, (TOK, LANES), 1) < PROJ
    out = []
    for k in range(2):
        picked = jnp.zeros((TOK, LANES), jnp.float32)
        for a in range(sub):
            for pair in range(len(experts) // 2):
                even, odd = experts[2 * pair], experts[2 * pair + 1]
                wanted = jnp.where(
                    low,
                    jnp.where(even[1] == a, even[0], -1),
                    jnp.where(odd[1] == a, odd[0], -1),
                ).astype(jnp.float32)
                picked += jnp.where(routes[:, k : k + 1] == wanted, total(a, pair), 0.0)
        out.append(picked + pltpu.roll(picked, PROJ, 1))
    return out


def right_sums(sub, width, toks, pieces):
    table = jnp.concatenate([p[:, :width] for p in pieces], axis=0)
    return [nt(toks[:, a * width : (a + 1) * width], table) for a in range(sub)]


def left_sums(sub, width, toks, pieces):
    table = jnp.concatenate([p[:, width:] for p in pieces], axis=0)
    at, size = sub * width, table.shape[1]
    return [nt(toks[:, at + a * size : at + (a + 1) * size], table) for a in range(sub)]


def picks(rows, tables, experts, width, sub):
    toks = jnp.concatenate(rows, axis=0)
    right, left = right_sums(sub, width, toks, tables), left_sums(sub, width, toks, tables)
    low = lax.broadcasted_iota(jnp.int32, (TOK, LANES), 1) < PROJ
    picked = []
    for b in range(len(rows)):
        here = slice(b * TOK, (b + 1) * TOK)
        named = toks[here, -LANES:].astype(jnp.float32)

        def pick_of(sums):
            return pick(lambda a, pair: sums[a][here, pair * LANES : (pair + 1) * LANES], named, experts, sub)

        picked.append([jnp.where(low, x, y) for x, y in zip(pick_of(left), pick_of(right))])
    return picked


def early_kernel(sub, width, ids, sizes, own, other, x, *refs):
    experts = [piece_of(at, sizes) for at in ids]
    rows = [own[...], other[...], x[...]]
    for b, slots in enumerate(picks(rows, refs[:-1], experts, width, sub)):
        for k, got in enumerate(slots):
            refs[-1][b, :, k * LANES : (k + 1) * LANES] = got


def mid_kernel(sub, width, ids, sizes, xc, *refs):
    experts = [piece_of(at, sizes) for at in ids]
    for k, got in enumerate(picks([xc[...]], refs[:-1], experts, width, sub)[0]):
        refs[-1][:, k * LANES : (k + 1) * LANES] = got


def last_kernel(sub, width, ids, sizes, own, other, x, xc, piece0, piece1, early_ref, mid_ref, *outs):
    experts = [piece_of(at, sizes) for at in ids]
    rows = [own[...], other[...], x[...], xc[...]]
    for b, slots in enumerate(picks(rows, (piece0, piece1), experts, width, sub)):
        for k, got in enumerate(slots):
            lanes = slice(k * LANES, (k + 1) * LANES)
            outs[b][:, lanes] = (early_ref[b, :, lanes] if b < 3 else mid_ref[:, lanes]) + got


def pack_kernel(outputs, routes_ref, *refs):
    core, _, half = position()
    n_blocks = sum(len(blocks) for blocks in outputs)
    ins, outs = refs[:n_blocks], refs[n_blocks : n_blocks + len(outputs)]
    buffers, in_sems, out_sems = refs[n_blocks + len(outputs) : -2], refs[-2], refs[-1]
    copies, i = [], 0
    for blocks, buffer in zip(outputs, buffers):
        at, group = 0, []
        for width, place, offset in blocks:
            start = pl.multiple_of((place(core, half) + offset) * width, LANES)
            copy = pltpu.make_async_copy(
                ins[i].at[:, pl.ds(start, width)], buffer.at[:, at : at + width], in_sems.at[i]
            )
            copy.start()
            group.append(copy)
            at, i = at + width, i + 1
        copies.append(group)
    row = lax.broadcasted_iota(jnp.int32, (TOK, LANES), 0)
    routes = routes_ref[...].astype(jnp.float32)
    named = jnp.where(row == 0, routes[0:1], jnp.where(row == 1, routes[1:2], 0.0))
    named = jnp.transpose(named).astype(jnp.bfloat16)
    back = []
    for i, (blocks, buffer, group) in enumerate(zip(outputs, buffers, copies)):
        size = sum(block[0] for block in blocks)
        if buffer.shape[1] > size:
            buffer[:, size:] = named
        for copy in group:
            copy.wait()
        copy = pltpu.make_async_copy(buffer, outs[i], out_sems.at[i])
        copy.start()
        back.append(copy)
    for copy in back:
        copy.wait()


def pack(routes, outputs, name):
    blocks = [b for out in outputs for b in out]
    shapes = []
    for out in outputs:
        rows = out[0][0].shape[0]
        shapes.append((rows, sum(b[1] for b in out) + (LANES if rows == TOK else 0)))
    hbm = pl.BlockSpec(memory_space=pl.ANY)
    return pl.pallas_call(
        functools.partial(pack_kernel, [[b[1:] for b in out] for out in outputs]),
        in_specs=[pl.BlockSpec(memory_space=pltpu.VMEM)] + [hbm] * len(blocks),
        out_specs=[hbm] * len(shapes),
        out_shape=[jax.ShapeDtypeStruct(x, jnp.bfloat16) for x in shapes],
        scratch_shapes=[pltpu.VMEM(x, jnp.bfloat16) for x in shapes]
        + [pltpu.SemaphoreType.DMA((len(blocks),)), pltpu.SemaphoreType.DMA((len(shapes),))],
        compiler_params=pltpu.CompilerParams(vmem_limit_bytes=2 * VMEM),
        name=name,
    )(routes, *[b[0] for b in blocks])


def local(kernel, name, out_shape, operands):
    vmem = pl.BlockSpec(memory_space=pltpu.VMEM)
    return pl.pallas_call(
        kernel,
        in_specs=[vmem] * len(operands),
        out_specs=jax.tree.map(lambda _: vmem, out_shape),
        out_shape=out_shape,
        compiler_params=pltpu.CompilerParams(vmem_limit_bytes=VMEM),
        name=name,
    )(*operands)


def gram_kernel(p0, p1, p2, p3, routes_ref, out_ref, flat):
    total = (p0[...] + p1[...]) + (p2[...] + p3[...])
    first, second = total[:, :LANES], total[:, LANES:]
    left = jnp.concatenate([jnp.transpose(first)[:PROJ], jnp.transpose(second)[:PROJ]], axis=1)
    right = jnp.concatenate([first, second], axis=0)
    named = routes_ref[...]
    rows = jnp.concatenate([jnp.where(named == e, left, 0.0) for e in range(EXPERTS)], axis=0)
    grams = lax.dot_general(
        rows,
        right,
        (((1,), (0,)), ((), ())),
        precision=lax.Precision.HIGHEST,
        preferred_element_type=jnp.float32,
    )
    grams = grams * (TOK**-0.5)
    low = lax.broadcasted_iota(jnp.int32, (PROJ // 2, LANES), 1) < PROJ
    for e in range(EXPERTS):
        top = grams[e * PROJ : e * PROJ + PROJ // 2]
        bottom = grams[e * PROJ + PROJ // 2 : (e + 1) * PROJ]
        flat[:, e, :] = jnp.where(low, pltpu.roll(top, PROJ, 1), bottom)
    mine = flat[...].reshape(PROJ // 4, 2 * EXPERTS, LANES).astype(jnp.bfloat16)
    for j in range(out_ref.shape[0]):
        out_ref[j] = mine


def gram(parts, routes, copies):
    return pl.pallas_call(
        gram_kernel,
        out_shape=jax.ShapeDtypeStruct((copies, PROJ // 4, 2 * EXPERTS, LANES), jnp.bfloat16),
        scratch_shapes=[pltpu.VMEM((PROJ // 2, EXPERTS, LANES), jnp.float32)],
        compiler_params=pltpu.CompilerParams(vmem_limit_bytes=2 * VMEM),
        name="gram",
    )(*parts, routes)


def fisher_kernel(own, other, fisher, out_ref):
    n = 2 * own.shape[0]
    core, _, _ = position()
    total = jnp.zeros((n * EXPERTS, fisher.shape[1]), jnp.float32)
    for i in range(PROJ // 4):
        rows = jnp.concatenate([x[:, i].astype(jnp.float32) for x in (own, other)], axis=0)
        rows = rows.reshape(n, 2, EXPERTS, LANES)
        for h in range(2):
            p = 2 * i + h
            table = jnp.concatenate(
                [
                    fisher[p * PROJ : (p + 1) * PROJ, :],
                    fisher[(PROJ // 2 + p) * PROJ : (PROJ // 2 + p + 1) * PROJ, :],
                ],
                axis=0,
            )
            lhs = rows[:, h].reshape(n * EXPERTS, LANES).astype(jnp.bfloat16)
            total += jnp.dot(lhs, table, preferred_element_type=jnp.float32)
    for j in range(n // 2):
        out_ref[2 * j + core] = total[j * EXPERTS : (j + 1) * EXPERTS]
        out_ref[2 * j + 1 - core] = total[(n // 2 + j) * EXPERTS : (n // 2 + j + 1) * EXPERTS]


def shards(features, grads, routes, proj_in, proj_out, fisher_inverse):
    groups, n = lax.axis_size("groups"), lax.axis_size("dp")
    chips = n // 2
    slices = n // EXPERTS
    sub = slices // 2
    y_size = 2 if groups == 2 else 1
    z_size = chips // y_size
    def move(x, to):
        pairs = []
        for g in range(groups):
            for d in range(n):
                tg, td = to(g, d)
                pairs.append((g * n + d, tg * n + td))
        return lax.ppermute(x, AXES, pairs)

    def to_core(g, d):
        return g, d ^ 1

    def to_x(g, d):
        return g ^ 1, d

    def to_x_core(g, d):
        return g ^ 1, d ^ 1

    def to_y(g, d):
        return g, d ^ 2

    def to_z(g, d):
        return g, (d + 2 * y_size) % n

    def from_z(g, d):
        return g, (d - 2 * y_size) % n

    quarter_in, quarter_out = proj_in.shape[1] // 2, proj_out.shape[1] // 2

    def after(x, *others):
        return lax.optimization_barrier((x, *others))[0]

    def whole(place):
        return [(grads, quarter_out, place, 4 * a) for a in range(sub)] + [
            (features, quarter_in, place, 4 * a) for a in range(sub)
        ]

    def by_half(core, half):
        return half

    routes = routes.T
    table, send_other, send_x = pack(
        routes,
        [
            [(proj_out, quarter_out, by_half, 0), (proj_in, quarter_in, by_half, 0)],
            whole(lambda core, half: 2 * (1 - core) + half),
            whole(lambda core, half: 2 * core + 1 - half),
        ],
        "pack_first",
    )
    send_xc, own = pack(
        after(routes, send_x),
        [whole(lambda core, half: 2 * (1 - core) + 1 - half), whole(lambda core, half: 2 * core + half)],
        "pack_second",
    )

    facing = move(table, to_y) if y_size == 2 else table
    other, x = move(send_other, to_core), move(send_x, to_x)
    xc = move(after(send_xc, facing), to_x_core)
    blocks, ids = [table], [0]
    ups, downs = z_size // 2, (z_size - 1) // 2
    up = down = table
    for k in range(1, ups + 1):
        up = move(after(up, facing, other) if k == 2 else up, to_z)
        blocks.append(up)
        ids.append(-k)
        if k <= downs:
            down = move(down, from_z)
            blocks.append(down)
            ids.append(k)
    pieces, where = [], []
    for i, block in enumerate(blocks):
        for across in range(y_size):
            if across:
                if i == 1:
                    block = after(block, facing)
                if i == len(blocks) - 1:
                    block = after(block, x, pieces[3])
                block = move(block, to_y) if i else facing
            pieces.append(block)
            where.append((ids[i] % z_size, across))

    f32 = jnp.float32
    sizes = (z_size, y_size, slices)
    early = local(
        functools.partial(early_kernel, sub, quarter_out, where[:-2], sizes),
        "project_early",
        jax.ShapeDtypeStruct((3, TOK, 2 * LANES), f32),
        [own, other, x] + pieces[:-2],
    )
    mid = local(
        functools.partial(mid_kernel, sub, quarter_out, where[:-2], sizes),
        "project_mid",
        jax.ShapeDtypeStruct((TOK, 2 * LANES), f32),
        [after(xc, early)] + pieces[:-2],
    )
    partial = local(
        functools.partial(last_kernel, sub, quarter_out, where[-2:], sizes),
        "project_last",
        [jax.ShapeDtypeStruct((TOK, 2 * LANES), f32)] * 4,
        [own, other, x, xc] + pieces[-2:] + [early, mid],
    )
    sums = [partial[0], move(partial[1], to_core), move(partial[2], to_x), move(partial[3], to_x_core)]
    mine = gram(sums, routes.reshape(1, -1), chips)

    same_core = [list(range(c, n, 2)) for c in range(2)]
    grams = lax.all_to_all(mine, "dp", split_axis=0, concat_axis=0, axis_index_groups=same_core, tiled=True)
    columns = local(
        fisher_kernel,
        "precondition",
        jax.ShapeDtypeStruct((n, EXPERTS, fisher_inverse.shape[1]), f32),
        [grams, move(grams, to_core), fisher_inverse],
    )
    result = lax.all_to_all(columns, "dp", split_axis=0, concat_axis=0, tiled=True)
    return jnp.transpose(result, (1, 0, 2)).reshape(1, EXPERTS, PROJ * PROJ)


def solution(mesh):
    in_specs = (
        P(AXES, None),
        P(AXES, None),
        P(AXES, None),
        P(None, "dp"),
        P(None, "dp"),
        P(None, "dp"),
    )
    out_specs = P(AXES, None, None)
    return jax.shard_map(shards, mesh=mesh, in_specs=in_specs, out_specs=out_specs, check_vma=False)
```

```python
import functools

import jax
import jax.numpy as jnp
from jax import lax
from jax.experimental import pallas as pl
from jax.experimental.pallas import tpu as pltpu
from jax.sharding import PartitionSpec as P

EXPERTS = 8
PROJ = 64
TOK = 128
LANES = 128
VMEM = 28 * 1024 * 1024
AXES = ("groups", "dp")


def position():
    place = lax.axis_index("dp")
    return lax.rem(place, 2), lax.div(place, 2), lax.rem(lax.axis_index("groups"), 2)


def piece_of(at, sizes):
    z_size, y_size, slices = sizes
    _, chip, _ = position()
    z, y = lax.div(chip, y_size), lax.rem(chip, y_size)
    step, across = at
    first = 2 * (lax.rem(z + (step + z_size), z_size) * y_size + (1 - y if across else y))
    return lax.div(first, slices), lax.div(lax.rem(first, slices), 2)


def nt(rows, table):
    return lax.dot_general(rows, table, (((1,), (1,)), ((), ())), preferred_element_type=jnp.float32)


def pick(total, routes, experts, sub):
    low = lax.broadcasted_iota(jnp.int32, (TOK, LANES), 1) < PROJ
    out = []
    for k in range(2):
        picked = jnp.zeros((TOK, LANES), jnp.float32)
        for a in range(sub):
            for pair in range(len(experts) // 2):
                even, odd = experts[2 * pair], experts[2 * pair + 1]
                wanted = jnp.where(
                    low,
                    jnp.where(even[1] == a, even[0], -1),
                    jnp.where(odd[1] == a, odd[0], -1),
                ).astype(jnp.float32)
                picked += jnp.where(routes[:, k : k + 1] == wanted, total(a, pair), 0.0)
        out.append(picked + pltpu.roll(picked, PROJ, 1))
    return out


def right_sums(sub, width, toks, pieces):
    table = jnp.concatenate([p[:, :width] for p in pieces], axis=0)
    return [nt(toks[:, a * width : (a + 1) * width], table) for a in range(sub)]


def left_sums(sub, width, toks, pieces):
    table = jnp.concatenate([p[:, width:] for p in pieces], axis=0)
    at, size = sub * width, table.shape[1]
    return [nt(toks[:, at + a * size : at + (a + 1) * size], table) for a in range(sub)]


def picks(rows, tables, experts, width, sub):
    toks = jnp.concatenate(rows, axis=0)
    right, left = right_sums(sub, width, toks, tables), left_sums(sub, width, toks, tables)
    low = lax.broadcasted_iota(jnp.int32, (TOK, LANES), 1) < PROJ
    picked = []
    for b in range(len(rows)):
        here = slice(b * TOK, (b + 1) * TOK)
        named = toks[here, -LANES:].astype(jnp.float32)

        def pick_of(sums):
            return pick(lambda a, pair: sums[a][here, pair * LANES : (pair + 1) * LANES], named, experts, sub)

        picked.append([jnp.where(low, x, y) for x, y in zip(pick_of(left), pick_of(right))])
    return picked


def early_kernel(sub, width, ids, sizes, own, other, x, *refs):
    experts = [piece_of(at, sizes) for at in ids]
    rows = [own[...], other[...], x[...]]
    for b, slots in enumerate(picks(rows, refs[:-1], experts, width, sub)):
        for k, got in enumerate(slots):
            refs[-1][b, :, k * LANES : (k + 1) * LANES] = got


def mid_kernel(sub, width, ids, sizes, xc, *refs):
    experts = [piece_of(at, sizes) for at in ids]
    for k, got in enumerate(picks([xc[...]], refs[:-1], experts, width, sub)[0]):
        refs[-1][:, k * LANES : (k + 1) * LANES] = got


def last_kernel(sub, width, ids, sizes, own, other, x, xc, early_ref, mid_ref, *refs):
    pieces, outs = refs[:-4], refs[-4:]
    experts = [piece_of(at, sizes) for at in ids]
    rows = [own[...], other[...], x[...], xc[...]]
    for b, slots in enumerate(picks(rows, pieces, experts, width, sub)):
        for k, got in enumerate(slots):
            lanes = slice(k * LANES, (k + 1) * LANES)
            outs[b][:, lanes] = (early_ref[b, :, lanes] if b < 3 else mid_ref[:, lanes]) + got


def pack_kernel(outputs, routes_ref, *refs):
    core, _, half = position()
    n_blocks = sum(len(blocks) for blocks in outputs)
    ins, outs = refs[:n_blocks], refs[n_blocks : n_blocks + len(outputs)]
    buffers, in_sems, out_sems = refs[n_blocks + len(outputs) : -2], refs[-2], refs[-1]
    copies, i = [], 0
    for blocks, buffer in zip(outputs, buffers):
        at, group = 0, []
        for width, place, offset in blocks:
            start = pl.multiple_of((place(core, half) + offset) * width, LANES)
            copy = pltpu.make_async_copy(
                ins[i].at[:, pl.ds(start, width)], buffer.at[:, at : at + width], in_sems.at[i]
            )
            copy.start()
            group.append(copy)
            at, i = at + width, i + 1
        copies.append(group)
    row = lax.broadcasted_iota(jnp.int32, (TOK, LANES), 0)
    routes = routes_ref[...].astype(jnp.float32)
    named = jnp.where(row == 0, routes[0:1], jnp.where(row == 1, routes[1:2], 0.0))
    named = jnp.transpose(named).astype(jnp.bfloat16)
    back = []
    for i, (blocks, buffer, group) in enumerate(zip(outputs, buffers, copies)):
        size = sum(block[0] for block in blocks)
        if buffer.shape[1] > size:
            buffer[:, size:] = named
        for copy in group:
            copy.wait()
        copy = pltpu.make_async_copy(buffer, outs[i], out_sems.at[i])
        copy.start()
        back.append(copy)
    for copy in back:
        copy.wait()


def pack(routes, outputs, name):
    blocks = [b for out in outputs for b in out]
    shapes = []
    for out in outputs:
        rows = out[0][0].shape[0]
        shapes.append((rows, sum(b[1] for b in out) + (LANES if rows == TOK else 0)))
    hbm = pl.BlockSpec(memory_space=pl.ANY)
    return pl.pallas_call(
        functools.partial(pack_kernel, [[b[1:] for b in out] for out in outputs]),
        in_specs=[pl.BlockSpec(memory_space=pltpu.VMEM)] + [hbm] * len(blocks),
        out_specs=[hbm] * len(shapes),
        out_shape=[jax.ShapeDtypeStruct(x, jnp.bfloat16) for x in shapes],
        scratch_shapes=[pltpu.VMEM(x, jnp.bfloat16) for x in shapes]
        + [pltpu.SemaphoreType.DMA((len(blocks),)), pltpu.SemaphoreType.DMA((len(shapes),))],
        compiler_params=pltpu.CompilerParams(vmem_limit_bytes=2 * VMEM),
        name=name,
    )(routes, *[b[0] for b in blocks])


def local(kernel, name, out_shape, operands):
    vmem = pl.BlockSpec(memory_space=pltpu.VMEM)
    return pl.pallas_call(
        kernel,
        in_specs=[vmem] * len(operands),
        out_specs=jax.tree.map(lambda _: vmem, out_shape),
        out_shape=out_shape,
        compiler_params=pltpu.CompilerParams(vmem_limit_bytes=VMEM),
        name=name,
    )(*operands)


def gram_kernel(p0, p1, p2, p3, routes_ref, out_ref):
    total = (p0[...] + p1[...]) + (p2[...] + p3[...])
    first, second = total[:, :LANES], total[:, LANES:]
    left = jnp.concatenate([jnp.transpose(first)[:PROJ], jnp.transpose(second)[:PROJ]], axis=1)
    right = jnp.concatenate([first, second], axis=0)
    left_high, right_high = left.astype(jnp.bfloat16).astype(jnp.float32), right.astype(jnp.bfloat16)
    left_low, right_low = left - left_high, (right - right_high.astype(jnp.float32)).astype(jnp.bfloat16)
    expert = lax.broadcasted_iota(jnp.int32, (EXPERTS, 2 * TOK), 0)
    chosen = jnp.where(jnp.broadcast_to(routes_ref[...], expert.shape) == expert, 1.0, 0.0)

    def masked(x):
        rows = [x[p : p + 1] * chosen for p in range(PROJ)]
        return jnp.concatenate(rows, axis=0).astype(jnp.bfloat16)

    high, low = masked(left_high), masked(left_low)
    grams = jnp.dot(high, right_high, preferred_element_type=jnp.float32)
    grams += jnp.dot(high, right_low, preferred_element_type=jnp.float32)
    grams += jnp.dot(low, right_high, preferred_element_type=jnp.float32)
    grams = grams * (TOK**-0.5)
    rows = PROJ // 2 * EXPERTS
    first = lax.broadcasted_iota(jnp.int32, (rows, LANES), 1) < PROJ
    mine = jnp.where(first, pltpu.roll(grams[:rows], PROJ, 1), grams[rows:])
    mine = mine.reshape(PROJ // 4, 2 * EXPERTS, LANES).astype(jnp.bfloat16)
    for j in range(out_ref.shape[0]):
        out_ref[j] = mine


def gram(parts, routes, copies):
    return pl.pallas_call(
        gram_kernel,
        out_shape=jax.ShapeDtypeStruct((copies, PROJ // 4, 2 * EXPERTS, LANES), jnp.bfloat16),
        compiler_params=pltpu.CompilerParams(vmem_limit_bytes=2 * VMEM),
        name="gram",
    )(*parts, routes)


def fisher_kernel(own, other, fisher, out_ref):
    n = 2 * own.shape[0]
    core, _, _ = position()
    total = jnp.zeros((n * EXPERTS, fisher.shape[1]), jnp.float32)
    for i in range(PROJ // 4):
        rows = jnp.concatenate([x[:, i].astype(jnp.float32) for x in (own, other)], axis=0)
        rows = rows.reshape(n, 2, EXPERTS, LANES)
        for h in range(2):
            p = 2 * i + h
            table = jnp.concatenate(
                [
                    fisher[p * PROJ : (p + 1) * PROJ, :],
                    fisher[(PROJ // 2 + p) * PROJ : (PROJ // 2 + p + 1) * PROJ, :],
                ],
                axis=0,
            )
            lhs = rows[:, h].reshape(n * EXPERTS, LANES).astype(jnp.bfloat16)
            total += jnp.dot(lhs, table, preferred_element_type=jnp.float32)
    width = fisher.shape[1]
    for j in range(n // 2):
        for rows, place in ((j, 2 * j + core), (n // 2 + j, 2 * j + 1 - core)):
            at = pl.multiple_of(place * width, LANES)
            out_ref[:, pl.ds(at, width)] = total[rows * EXPERTS : (rows + 1) * EXPERTS]


def shards(features, grads, routes, proj_in, proj_out, fisher_inverse):
    groups, n = lax.axis_size("groups"), lax.axis_size("dp")
    chips = n // 2
    slices = n // EXPERTS
    sub = slices // 2
    y_size = 2 if groups == 2 else 1
    z_size = chips // y_size
    def move(x, to):
        pairs = []
        for g in range(groups):
            for d in range(n):
                tg, td = to(g, d)
                pairs.append((g * n + d, tg * n + td))
        return lax.ppermute(x, AXES, pairs)

    def to_core(g, d):
        return g, d ^ 1

    def to_x(g, d):
        return g ^ 1, d

    def to_x_core(g, d):
        return g ^ 1, d ^ 1

    def to_y(g, d):
        return g, d ^ 2

    def to_z(g, d):
        return g, (d + 2 * y_size) % n

    def from_z(g, d):
        return g, (d - 2 * y_size) % n

    quarter_in, quarter_out = proj_in.shape[1] // 2, proj_out.shape[1] // 2

    def after(x, *others):
        return lax.optimization_barrier((x, *others))[0]

    def whole(place):
        return [(grads, quarter_out, place, 4 * a) for a in range(sub)] + [
            (features, quarter_in, place, 4 * a) for a in range(sub)
        ]

    def by_half(core, half):
        return half

    routes = routes.T
    table, send_other, send_x = pack(
        routes,
        [
            [(proj_out, quarter_out, by_half, 0), (proj_in, quarter_in, by_half, 0)],
            whole(lambda core, half: 2 * (1 - core) + half),
            whole(lambda core, half: 2 * core + 1 - half),
        ],
        "pack_first",
    )
    send_xc, own = pack(
        after(routes, send_x),
        [whole(lambda core, half: 2 * (1 - core) + 1 - half), whole(lambda core, half: 2 * core + half)],
        "pack_second",
    )

    facing = move(table, to_y) if y_size == 2 else table
    other, x = move(send_other, to_core), move(send_x, to_x)
    xc = move(after(send_xc, facing), to_x_core)
    blocks, ids = [table], [0]
    ups, downs = z_size // 2, (z_size - 1) // 2
    up = down = table
    for k in range(1, ups + 1):
        up = move(after(up, facing, other) if k == 2 else up, to_z)
        blocks.append(up)
        ids.append(-k)
        if k <= downs:
            down = move(down, from_z)
            blocks.append(down)
            ids.append(k)
    pieces, where = [], []
    for i, block in enumerate(blocks):
        for across in range(y_size):
            if across:
                if i == 1:
                    block = after(block, facing)
                block = facing if i == 0 else block
                if 0 < i < len(blocks) - 1:
                    block = move(block, to_y)
                if i == len(blocks) - 1:
                    near = move(after(block, x, pieces[3])[: PROJ // 2], to_y)
                    block = (near, move(pieces[3][PROJ // 2 :], to_z))
            pieces.append(block)
            where.append((ids[i] % z_size, across))

    f32 = jnp.float32
    sizes = (z_size, y_size, slices)
    early = local(
        functools.partial(early_kernel, sub, quarter_out, where[:-2], sizes),
        "project_early",
        jax.ShapeDtypeStruct((3, TOK, 2 * LANES), f32),
        [own, other, x] + pieces[:-2],
    )
    mid = local(
        functools.partial(mid_kernel, sub, quarter_out, where[:-2], sizes),
        "project_mid",
        jax.ShapeDtypeStruct((TOK, 2 * LANES), f32),
        [after(xc, early)] + pieces[:-2],
    )
    partial = local(
        functools.partial(last_kernel, sub, quarter_out, where[-2:], sizes),
        "project_last",
        [jax.ShapeDtypeStruct((TOK, 2 * LANES), f32)] * 4,
        [own, other, x, xc, early, mid] + jax.tree.leaves(pieces[-2:]),
    )
    sums = [partial[0], move(partial[1], to_core), move(partial[2], to_x), move(partial[3], to_x_core)]
    mine = gram(sums, routes.reshape(1, -1), chips)

    same_core = [list(range(c, n, 2)) for c in range(2)]
    grams = lax.all_to_all(mine, "dp", split_axis=0, concat_axis=0, axis_index_groups=same_core, tiled=True)
    columns = local(
        fisher_kernel,
        "precondition",
        jax.ShapeDtypeStruct((EXPERTS, PROJ * PROJ), f32),
        [grams, move(grams, to_core), fisher_inverse],
    )
    result = lax.all_to_all(columns, "dp", split_axis=1, concat_axis=1, tiled=True)
    return result.reshape(1, EXPERTS, PROJ * PROJ)


def solution(mesh):
    in_specs = (
        P(AXES, None),
        P(AXES, None),
        P(AXES, None),
        P(None, "dp"),
        P(None, "dp"),
        P(None, "dp"),
    )
    out_specs = P(AXES, None, None)
    return jax.shard_map(shards, mesh=mesh, in_specs=in_specs, out_specs=out_specs, check_vma=False)
```

```python
import functools

import jax
import jax.numpy as jnp
from jax import lax
from jax.experimental import pallas as pl
from jax.experimental.pallas import tpu as pltpu
from jax.sharding import PartitionSpec as P

EXPERTS = 8
PROJ = 64
TOK = 128
LANES = 128
VMEM = 28 * 1024 * 1024
AXES = ("groups", "dp")


def position():
    place = lax.axis_index("dp")
    return lax.rem(place, 2), lax.div(place, 2), lax.rem(lax.axis_index("groups"), 2)


def piece_of(at, sizes):
    z_size, y_size, slices = sizes
    _, chip, _ = position()
    z, y = lax.div(chip, y_size), lax.rem(chip, y_size)
    step, across = at
    first = 2 * (lax.rem(z + (step + z_size), z_size) * y_size + (1 - y if across else y))
    return lax.div(first, slices), lax.div(lax.rem(first, slices), 2)


def nt(rows, table):
    return lax.dot_general(rows, table, (((1,), (1,)), ((), ())), preferred_element_type=jnp.float32)


def pick(total, routes, experts, sub):
    low = lax.broadcasted_iota(jnp.int32, (TOK, LANES), 1) < PROJ
    out = []
    for k in range(2):
        picked = jnp.zeros((TOK, LANES), jnp.float32)
        for a in range(sub):
            for pair in range(len(experts) // 2):
                even, odd = experts[2 * pair], experts[2 * pair + 1]
                wanted = jnp.where(
                    low,
                    jnp.where(even[1] == a, even[0], -1),
                    jnp.where(odd[1] == a, odd[0], -1),
                ).astype(jnp.float32)
                picked += jnp.where(routes[:, k : k + 1] == wanted, total(a, pair), 0.0)
        out.append(picked + pltpu.roll(picked, PROJ, 1))
    return out


def right_sums(sub, width, toks, pieces):
    table = jnp.concatenate([p[:, :width] for p in pieces], axis=0)
    return [nt(toks[:, a * width : (a + 1) * width], table) for a in range(sub)]


def left_sums(sub, width, toks, pieces):
    table = jnp.concatenate([p[:, width:] for p in pieces], axis=0)
    at, size = sub * width, table.shape[1]
    return [nt(toks[:, at + a * size : at + (a + 1) * size], table) for a in range(sub)]


def picks(rows, tables, experts, width, sub):
    toks = jnp.concatenate(rows, axis=0)
    right, left = right_sums(sub, width, toks, tables), left_sums(sub, width, toks, tables)
    low = lax.broadcasted_iota(jnp.int32, (TOK, LANES), 1) < PROJ
    picked = []
    for b in range(len(rows)):
        here = slice(b * TOK, (b + 1) * TOK)
        named = toks[here, -LANES:].astype(jnp.float32)

        def pick_of(sums):
            return pick(lambda a, pair: sums[a][here, pair * LANES : (pair + 1) * LANES], named, experts, sub)

        picked.append([jnp.where(low, x, y) for x, y in zip(pick_of(left), pick_of(right))])
    return picked


def early_kernel(sub, width, ids, sizes, own, other, x, *refs):
    experts = [piece_of(at, sizes) for at in ids]
    rows = [own[...], other[...], x[...]]
    for b, slots in enumerate(picks(rows, refs[:-1], experts, width, sub)):
        for k, got in enumerate(slots):
            refs[-1][b, :, k * LANES : (k + 1) * LANES] = got


def late_kernel(sub, width, ids, sizes, own, other, x, early_ref, *refs):
    pieces, outs = refs[:-3], refs[-3:]
    experts = [piece_of(at, sizes) for at in ids]
    rows = [own[...], other[...], x[...]]
    for b, slots in enumerate(picks(rows, pieces, experts, width, sub)):
        for k, got in enumerate(slots):
            lanes = slice(k * LANES, (k + 1) * LANES)
            outs[b][:, lanes] = early_ref[b, :, lanes] + got


def last_kernel(sub, width, ids, sizes, xc, *refs):
    experts = [piece_of(at, sizes) for at in ids]
    for k, got in enumerate(picks([xc[...]], refs[:-1], experts, width, sub)[0]):
        refs[-1][:, k * LANES : (k + 1) * LANES] = got


def pack_kernel(outputs, routes_ref, *refs):
    core, _, half = position()
    n_blocks = sum(len(blocks) for blocks in outputs)
    ins, outs, routes, sems = refs[:n_blocks], refs[n_blocks:-2], refs[-2], refs[-1]
    copies, i = [], 0
    named = pltpu.make_async_copy(routes_ref, routes, sems.at[n_blocks])
    named.start()
    for blocks, out in zip(outputs, outs):
        at = 0
        for width, place, offset in blocks:
            start = pl.multiple_of((place(core, half) + offset) * width, LANES)
            copy = pltpu.make_async_copy(ins[i].at[:, pl.ds(start, width)], out.at[:, at : at + width], sems.at[i])
            copy.start()
            copies.append(copy)
            at, i = at + width, i + 1
    row = lax.broadcasted_iota(jnp.int32, (TOK, LANES), 0)
    named.wait()
    routes = routes[...].astype(jnp.float32)
    named = jnp.where(row == 0, routes[0:1], jnp.where(row == 1, routes[1:2], 0.0))
    named = jnp.transpose(named).astype(jnp.bfloat16)
    for blocks, out in zip(outputs, outs):
        size = sum(block[0] for block in blocks)
        if out.shape[1] > size:
            out[:, size:] = named
    for copy in copies:
        copy.wait()


def pack(routes, outputs, name):
    blocks = [b for out in outputs for b in out]
    shapes = []
    for out in outputs:
        rows = out[0][0].shape[0]
        shapes.append((rows, sum(b[1] for b in out) + (LANES if rows == TOK else 0)))
    return pl.pallas_call(
        functools.partial(pack_kernel, [[b[1:] for b in out] for out in outputs]),
        in_specs=[pl.BlockSpec(memory_space=pltpu.HBM)] * (1 + len(blocks)),
        out_specs=[pl.BlockSpec(memory_space=pltpu.VMEM)] * len(shapes),
        out_shape=[jax.ShapeDtypeStruct(x, jnp.bfloat16) for x in shapes],
        scratch_shapes=[pltpu.VMEM((2, TOK), jnp.int32), pltpu.SemaphoreType.DMA((len(blocks) + 1,))],
        compiler_params=pltpu.CompilerParams(vmem_limit_bytes=VMEM),
        name=name,
    )(*[pltpu.with_memory_space_constraint(x, pltpu.HBM) for x in [routes] + [b[0] for b in blocks]])


def local(kernel, name, out_shape, operands):
    vmem = pl.BlockSpec(memory_space=pltpu.VMEM)
    return pl.pallas_call(
        kernel,
        in_specs=[vmem] * len(operands),
        out_specs=jax.tree.map(lambda _: vmem, out_shape),
        out_shape=out_shape,
        compiler_params=pltpu.CompilerParams(vmem_limit_bytes=VMEM),
        name=name,
    )(*operands)


def gram_kernel(p0, p1, p2, p3, routes_ref, out_ref):
    total = (p0[...] + p1[...]) + (p2[...] + p3[...])
    first, second = total[:, :LANES], total[:, LANES:]
    left = jnp.concatenate([jnp.transpose(first)[:PROJ], jnp.transpose(second)[:PROJ]], axis=1)
    right = jnp.concatenate([first, second], axis=0)
    left_high, right_high = left.astype(jnp.bfloat16).astype(jnp.float32), right.astype(jnp.bfloat16)
    left_low, right_low = left - left_high, (right - right_high.astype(jnp.float32)).astype(jnp.bfloat16)
    expert = lax.broadcasted_iota(jnp.int32, (EXPERTS, 2 * TOK), 0)
    chosen = jnp.where(jnp.broadcast_to(routes_ref[...], expert.shape) == expert, 1.0, 0.0)

    def masked(x):
        rows = [x[p : p + 1] * chosen for p in range(PROJ)]
        return jnp.concatenate(rows, axis=0).astype(jnp.bfloat16)

    high, low = masked(left_high), masked(left_low)
    grams = jnp.dot(high, right_high, preferred_element_type=jnp.float32)
    grams += jnp.dot(high, right_low, preferred_element_type=jnp.float32)
    grams += jnp.dot(low, right_high, preferred_element_type=jnp.float32)
    grams = grams * (TOK**-0.5)
    rows = PROJ // 2 * EXPERTS
    first = lax.broadcasted_iota(jnp.int32, (rows, LANES), 1) < PROJ
    mine = jnp.where(first, pltpu.roll(grams[:rows], PROJ, 1), grams[rows:])
    mine = mine.reshape(PROJ // 4, 2 * EXPERTS, LANES).astype(jnp.bfloat16)
    for j in range(out_ref.shape[0]):
        out_ref[j] = mine


def fisher_kernel(own, other, fisher, out_ref):
    n = 2 * own.shape[0]
    core, _, _ = position()
    total = jnp.zeros((n * EXPERTS, fisher.shape[1]), jnp.float32)
    for i in range(PROJ // 4):
        rows = jnp.concatenate([x[:, i].astype(jnp.float32) for x in (own, other)], axis=0)
        rows = rows.reshape(n, 2, EXPERTS, LANES)
        for h in range(2):
            p = 2 * i + h
            table = jnp.concatenate(
                [
                    fisher[p * PROJ : (p + 1) * PROJ, :],
                    fisher[(PROJ // 2 + p) * PROJ : (PROJ // 2 + p + 1) * PROJ, :],
                ],
                axis=0,
            )
            lhs = rows[:, h].reshape(n * EXPERTS, LANES).astype(jnp.bfloat16)
            total += jnp.dot(lhs, table, preferred_element_type=jnp.float32)
    width = fisher.shape[1]
    for j in range(n // 2):
        for rows, place in ((j, 2 * j + core), (n // 2 + j, 2 * j + 1 - core)):
            at = pl.multiple_of(place * width, LANES)
            out_ref[:, pl.ds(at, width)] = total[rows * EXPERTS : (rows + 1) * EXPERTS]


def shards(features, grads, routes, proj_in, proj_out, fisher_inverse):
    groups, n = lax.axis_size("groups"), lax.axis_size("dp")
    chips = n // 2
    slices = n // EXPERTS
    sub = slices // 2
    y_size = 2 if groups == 2 else 1
    z_size = chips // y_size
    def move(x, to):
        pairs = []
        for g in range(groups):
            for d in range(n):
                tg, td = to(g, d)
                pairs.append((g * n + d, tg * n + td))
        return lax.ppermute(x, AXES, pairs)

    def to_core(g, d):
        return g, d ^ 1

    def to_x(g, d):
        return g ^ 1, d

    def to_x_core(g, d):
        return g ^ 1, d ^ 1

    def to_y(g, d):
        return g, d ^ 2

    def to_z(g, d):
        return g, (d + 2 * y_size) % n

    def from_z(g, d):
        return g, (d - 2 * y_size) % n

    quarter_in, quarter_out = proj_in.shape[1] // 2, proj_out.shape[1] // 2

    def after(x, *others):
        return lax.optimization_barrier((x, *others))[0]

    def whole(place):
        return [(grads, quarter_out, place, 4 * a) for a in range(sub)] + [
            (features, quarter_in, place, 4 * a) for a in range(sub)
        ]

    def by_half(core, half):
        return half

    routes = routes.T
    table, send_other, send_x = pack(
        routes,
        [
            [(proj_out, quarter_out, by_half, 0), (proj_in, quarter_in, by_half, 0)],
            whole(lambda core, half: 2 * (1 - core) + half),
            whole(lambda core, half: 2 * core + 1 - half),
        ],
        "pack_first",
    )
    send_xc, own = pack(
        after(routes, send_x),
        [whole(lambda core, half: 2 * (1 - core) + 1 - half), whole(lambda core, half: 2 * core + half)],
        "pack_second",
    )

    facing = move(table, to_y) if y_size == 2 else table
    other, x = move(send_other, to_core), move(send_x, to_x)
    xc = move(after(send_xc, facing), to_x_core)
    blocks, ids = [table], [0]
    ups, downs = z_size // 2, (z_size - 1) // 2
    up = down = table
    for k in range(1, ups + 1):
        up = move(after(up, facing, other) if k == 2 else up, to_z)
        blocks.append(up)
        ids.append(-k)
        if k <= downs:
            down = move(down, from_z)
            blocks.append(down)
            ids.append(k)
    pieces, where = [], []
    for i, block in enumerate(blocks):
        for across in range(y_size):
            if across:
                if i == 1:
                    block = after(block, facing)
                block = facing if i == 0 else block
                if 0 < i < len(blocks) - 1:
                    block = move(block, to_y)
                if i == len(blocks) - 1:
                    near = move(after(block, x, pieces[3])[: PROJ // 2], to_y)
                    block = (near, move(pieces[3][PROJ // 2 :], to_z))
            pieces.append(block)
            where.append((ids[i] % z_size, across))

    f32 = jnp.float32
    sizes = (z_size, y_size, slices)
    early = local(
        functools.partial(early_kernel, sub, quarter_out, where[:-2], sizes),
        "project_early",
        jax.ShapeDtypeStruct((3, TOK, 2 * LANES), f32),
        [own, other, x] + pieces[:-2],
    )
    block = jax.ShapeDtypeStruct((TOK, 2 * LANES), f32)
    partial = local(
        functools.partial(late_kernel, sub, quarter_out, where[-2:], sizes),
        "project_late",
        [block] * 3,
        [own, other, x, early] + jax.tree.leaves(pieces[-2:]),
    )
    ending = local(
        functools.partial(last_kernel, sub, quarter_out, where, sizes),
        "project_last",
        block,
        [after(xc, partial[0])] + jax.tree.leaves(pieces),
    )
    sums = [partial[0], move(partial[1], to_core), move(partial[2], to_x), move(ending, to_x_core)]
    mine = local(
        gram_kernel,
        "gram",
        jax.ShapeDtypeStruct((chips, PROJ // 4, 2 * EXPERTS, LANES), jnp.bfloat16),
        sums + [routes.reshape(1, -1)],
    )

    same_core = [list(range(c, n, 2)) for c in range(2)]
    grams = lax.all_to_all(mine, "dp", split_axis=0, concat_axis=0, axis_index_groups=same_core, tiled=True)
    columns = local(
        fisher_kernel,
        "precondition",
        jax.ShapeDtypeStruct((EXPERTS, PROJ * PROJ), f32),
        [grams, move(grams, to_core), fisher_inverse],
    )
    result = lax.all_to_all(columns, "dp", split_axis=1, concat_axis=1, tiled=True)
    return result.reshape(1, EXPERTS, PROJ * PROJ)


def solution(mesh):
    in_specs = (
        P(AXES, None),
        P(AXES, None),
        P(AXES, None),
        P(None, "dp"),
        P(None, "dp"),
        P(None, "dp"),
    )
    out_specs = P(AXES, None, None)
    return jax.shard_map(shards, mesh=mesh, in_specs=in_specs, out_specs=out_specs, check_vma=False)
```

```python
import functools

import jax
import jax.numpy as jnp
from jax import lax
from jax.experimental import pallas as pl
from jax.experimental.pallas import tpu as pltpu
from jax.sharding import PartitionSpec as P

EXPERTS = 8
PROJ = 64
TOK = 128
LANES = 128
VMEM = 28 * 1024 * 1024
AXES = ("groups", "dp")


def position():
    place = lax.axis_index("dp")
    return lax.rem(place, 2), lax.div(place, 2), lax.rem(lax.axis_index("groups"), 2)


def piece_of(at, sizes):
    z_size, y_size, slices = sizes
    _, chip, _ = position()
    z, y = lax.div(chip, y_size), lax.rem(chip, y_size)
    step, across = at
    first = 2 * (lax.rem(z + (step + z_size), z_size) * y_size + (1 - y if across else y))
    return lax.div(first, slices), lax.div(lax.rem(first, slices), 2)


def nt(rows, table):
    return lax.dot_general(rows, table, (((1,), (1,)), ((), ())), preferred_element_type=jnp.float32)


def pick(total, routes, experts, sub):
    low = lax.broadcasted_iota(jnp.int32, (TOK, LANES), 1) < PROJ
    out = []
    for k in range(2):
        picked = jnp.zeros((TOK, LANES), jnp.float32)
        for a in range(sub):
            for pair in range(len(experts) // 2):
                even, odd = experts[2 * pair], experts[2 * pair + 1]
                wanted = jnp.where(
                    low,
                    jnp.where(even[1] == a, even[0], -1),
                    jnp.where(odd[1] == a, odd[0], -1),
                ).astype(jnp.float32)
                picked += jnp.where(routes[:, k : k + 1] == wanted, total(a, pair), 0.0)
        out.append(picked + pltpu.roll(picked, PROJ, 1))
    return out


def right_sums(sub, width, toks, pieces):
    table = jnp.concatenate([p[:, :width] for p in pieces], axis=0)
    return [nt(toks[:, a * width : (a + 1) * width], table) for a in range(sub)]


def left_sums(sub, width, toks, pieces):
    table = jnp.concatenate([p[:, width:] for p in pieces], axis=0)
    at, size = sub * width, table.shape[1]
    return [nt(toks[:, at + a * size : at + (a + 1) * size], table) for a in range(sub)]


def picks(rows, tables, experts, width, sub):
    toks = jnp.concatenate(rows, axis=0)
    right, left = right_sums(sub, width, toks, tables), left_sums(sub, width, toks, tables)
    low = lax.broadcasted_iota(jnp.int32, (TOK, LANES), 1) < PROJ
    picked = []
    for b in range(len(rows)):
        here = slice(b * TOK, (b + 1) * TOK)
        named = toks[here, -LANES:].astype(jnp.float32)

        def pick_of(sums):
            return pick(lambda a, pair: sums[a][here, pair * LANES : (pair + 1) * LANES], named, experts, sub)

        picked.append([jnp.where(low, x, y) for x, y in zip(pick_of(left), pick_of(right))])
    return picked


def early_kernel(sub, width, ids, sizes, own, other, x, *refs):
    experts = [piece_of(at, sizes) for at in ids]
    rows = [own[...], other[...], x[...]]
    for b, slots in enumerate(picks(rows, refs[:-1], experts, width, sub)):
        for k, got in enumerate(slots):
            refs[-1][b, :, k * LANES : (k + 1) * LANES] = got


def late_kernel(sub, width, ids, sizes, own, other, x, early_ref, *refs):
    pieces, outs = refs[:-3], refs[-3:]
    experts = [piece_of(at, sizes) for at in ids]
    rows = [own[...], other[...], x[...]]
    for b, slots in enumerate(picks(rows, pieces, experts, width, sub)):
        for k, got in enumerate(slots):
            lanes = slice(k * LANES, (k + 1) * LANES)
            outs[b][:, lanes] = early_ref[b, :, lanes] + got


def last_kernel(sub, width, ids, sizes, xc, *refs):
    experts = [piece_of(at, sizes) for at in ids]
    for k, got in enumerate(picks([xc[...]], refs[:-1], experts, width, sub)[0]):
        refs[-1][:, k * LANES : (k + 1) * LANES] = got


def pack_kernel(outputs, routes_ref, *refs):
    core, _, half = position()
    n_blocks = sum(len(blocks) for blocks in outputs)
    ins, outs, routes, sems = refs[:n_blocks], refs[n_blocks:-2], refs[-2], refs[-1]
    copies, i = [], 0
    named = pltpu.make_async_copy(routes_ref, routes, sems.at[n_blocks])
    named.start()
    for blocks, out in zip(outputs, outs):
        at = 0
        for width, place, offset in blocks:
            start = pl.multiple_of((place(core, half) + offset) * width, LANES)
            copy = pltpu.make_async_copy(ins[i].at[:, pl.ds(start, width)], out.at[:, at : at + width], sems.at[i])
            copy.start()
            copies.append(copy)
            at, i = at + width, i + 1
    row = lax.broadcasted_iota(jnp.int32, (TOK, LANES), 0)
    named.wait()
    routes = routes[...].astype(jnp.float32)
    named = jnp.where(row == 0, routes[0:1], jnp.where(row == 1, routes[1:2], 0.0))
    named = jnp.transpose(named).astype(jnp.bfloat16)
    for blocks, out in zip(outputs, outs):
        size = sum(block[0] for block in blocks)
        if out.shape[1] > size:
            out[:, size:] = named
    for copy in copies:
        copy.wait()


def pack(routes, outputs, name):
    blocks = [b for out in outputs for b in out]
    shapes = []
    for out in outputs:
        rows = out[0][0].shape[0]
        shapes.append((rows, sum(b[1] for b in out) + (LANES if rows == TOK else 0)))
    return pl.pallas_call(
        functools.partial(pack_kernel, [[b[1:] for b in out] for out in outputs]),
        in_specs=[pl.BlockSpec(memory_space=pltpu.HBM)] * (1 + len(blocks)),
        out_specs=[pl.BlockSpec(memory_space=pltpu.VMEM)] * len(shapes),
        out_shape=[jax.ShapeDtypeStruct(x, jnp.bfloat16) for x in shapes],
        scratch_shapes=[pltpu.VMEM((2, TOK), jnp.int32), pltpu.SemaphoreType.DMA((len(blocks) + 1,))],
        compiler_params=pltpu.CompilerParams(vmem_limit_bytes=VMEM),
        name=name,
    )(*[pltpu.with_memory_space_constraint(x, pltpu.HBM) for x in [routes] + [b[0] for b in blocks]])


def local(kernel, name, out_shape, operands):
    vmem = pl.BlockSpec(memory_space=pltpu.VMEM)
    return pl.pallas_call(
        kernel,
        in_specs=[vmem] * len(operands),
        out_specs=jax.tree.map(lambda _: vmem, out_shape),
        out_shape=out_shape,
        compiler_params=pltpu.CompilerParams(vmem_limit_bytes=VMEM),
        name=name,
    )(*operands)


def gram_kernel(p0, p1, p2, p3, routes_ref, out_ref):
    total = (p0[...] + p1[...]) + (p2[...] + p3[...])
    first, second = total[:, :LANES], total[:, LANES:]
    left = jnp.concatenate([jnp.transpose(first)[:PROJ], jnp.transpose(second)[:PROJ]], axis=1)
    right = jnp.concatenate([first, second], axis=0)
    left_high, right_high = left.astype(jnp.bfloat16).astype(jnp.float32), right.astype(jnp.bfloat16)
    left_low, right_low = left - left_high, (right - right_high.astype(jnp.float32)).astype(jnp.bfloat16)
    expert = lax.broadcasted_iota(jnp.int32, (EXPERTS, 2 * TOK), 0)
    chosen = jnp.where(jnp.broadcast_to(routes_ref[...], expert.shape) == expert, 1.0, 0.0)

    def masked(x):
        rows = [x[p : p + 1] * chosen for p in range(PROJ)]
        return jnp.concatenate(rows, axis=0).astype(jnp.bfloat16)

    high, low = masked(left_high), masked(left_low)
    grams = jnp.dot(high, right_high, preferred_element_type=jnp.float32)
    grams += jnp.dot(high, right_low, preferred_element_type=jnp.float32)
    grams += jnp.dot(low, right_high, preferred_element_type=jnp.float32)
    grams = grams * (TOK**-0.5)
    rows = PROJ // 2 * EXPERTS
    first = lax.broadcasted_iota(jnp.int32, (rows, LANES), 1) < PROJ
    mine = jnp.where(first, pltpu.roll(grams[:rows], PROJ, 1), grams[rows:])
    out_ref[...] = mine.reshape(PROJ // 4, 2 * EXPERTS, LANES).astype(jnp.bfloat16)


def fisher_kernel(steps, *refs):
    fisher, out_ref = refs[-2:]
    n = 2 * len(steps)
    core, chip, _ = position()
    total = jnp.zeros((n * EXPERTS, fisher.shape[1]), jnp.float32)
    for i in range(PROJ // 4):
        rows = jnp.concatenate([x[i].astype(jnp.float32).reshape(1, 2, EXPERTS, LANES) for x in refs[:n]], axis=0)
        for h in range(2):
            p = 2 * i + h
            table = jnp.concatenate(
                [
                    fisher[p * PROJ : (p + 1) * PROJ, :],
                    fisher[(PROJ // 2 + p) * PROJ : (PROJ // 2 + p + 1) * PROJ, :],
                ],
                axis=0,
            )
            lhs = rows[:, h].reshape(n * EXPERTS, LANES).astype(jnp.bfloat16)
            total += jnp.dot(lhs, table, preferred_element_type=jnp.float32)
    width = fisher.shape[1]
    for j in range(n):
        owner = 2 * jnp.bitwise_xor(chip, steps[j % len(steps)]) + (core if j < len(steps) else 1 - core)
        at = pl.multiple_of(owner * width, LANES)
        out_ref[:, pl.ds(at, width)] = total[j * EXPERTS : (j + 1) * EXPERTS]


def shards(features, grads, routes, proj_in, proj_out, fisher_inverse):
    groups, n = lax.axis_size("groups"), lax.axis_size("dp")
    chips = n // 2
    slices = n // EXPERTS
    sub = slices // 2
    y_size = 2 if groups == 2 else 1
    z_size = chips // y_size
    def move(x, to):
        pairs = []
        for g in range(groups):
            for d in range(n):
                tg, td = to(g, d)
                pairs.append((g * n + d, tg * n + td))
        return lax.ppermute(x, AXES, pairs)

    def to_core(g, d):
        return g, d ^ 1

    def to_x(g, d):
        return g ^ 1, d

    def to_x_core(g, d):
        return g ^ 1, d ^ 1

    def to_y(g, d):
        return g, d ^ 2

    def to_z(g, d):
        return g, (d + 2 * y_size) % n

    def from_z(g, d):
        return g, (d - 2 * y_size) % n

    quarter_in, quarter_out = proj_in.shape[1] // 2, proj_out.shape[1] // 2

    def after(x, *others):
        return lax.optimization_barrier((x, *others))[0]

    def whole(place):
        return [(grads, quarter_out, place, 4 * a) for a in range(sub)] + [
            (features, quarter_in, place, 4 * a) for a in range(sub)
        ]

    def by_half(core, half):
        return half

    routes = routes.T
    table, send_other, send_x = pack(
        routes,
        [
            [(proj_out, quarter_out, by_half, 0), (proj_in, quarter_in, by_half, 0)],
            whole(lambda core, half: 2 * (1 - core) + half),
            whole(lambda core, half: 2 * core + 1 - half),
        ],
        "pack_first",
    )
    send_xc, own = pack(
        after(routes, send_x),
        [whole(lambda core, half: 2 * (1 - core) + 1 - half), whole(lambda core, half: 2 * core + half)],
        "pack_second",
    )

    facing = move(table, to_y) if y_size == 2 else table
    other, x = move(send_other, to_core), move(send_x, to_x)
    xc = move(after(send_xc, facing), to_x_core)
    blocks, ids = [table], [0]
    ups, downs = z_size // 2, (z_size - 1) // 2
    up = down = table
    for k in range(1, ups + 1):
        up = move(after(up, facing, other) if k == 2 else up, to_z)
        blocks.append(up)
        ids.append(-k)
        if k <= downs:
            down = move(down, from_z)
            blocks.append(down)
            ids.append(k)
    pieces, where = [], []
    for i, block in enumerate(blocks):
        for across in range(y_size):
            if across:
                if i == 1:
                    block = after(block, facing)
                block = facing if i == 0 else block
                if 0 < i < len(blocks) - 1:
                    block = move(block, to_y)
                if i == len(blocks) - 1:
                    near = move(after(block, x, pieces[3])[: PROJ // 2], to_y)
                    block = (near, move(pieces[3][PROJ // 2 :], to_z))
            pieces.append(block)
            where.append((ids[i] % z_size, across))

    f32 = jnp.float32
    sizes = (z_size, y_size, slices)
    early = local(
        functools.partial(early_kernel, sub, quarter_out, where[:-2], sizes),
        "project_early",
        jax.ShapeDtypeStruct((3, TOK, 2 * LANES), f32),
        [own, other, x] + pieces[:-2],
    )
    block = jax.ShapeDtypeStruct((TOK, 2 * LANES), f32)
    partial = local(
        functools.partial(late_kernel, sub, quarter_out, where[-2:], sizes),
        "project_late",
        [block] * 3,
        [own, other, x, early] + jax.tree.leaves(pieces[-2:]),
    )
    ending = local(
        functools.partial(last_kernel, sub, quarter_out, where, sizes),
        "project_last",
        block,
        [after(xc, partial[0])] + jax.tree.leaves(pieces),
    )
    sums = [partial[0], move(partial[1], to_core), move(partial[2], to_x), move(ending, to_x_core)]
    mine = local(
        gram_kernel,
        "gram",
        jax.ShapeDtypeStruct((PROJ // 4, 2 * EXPERTS, LANES), jnp.bfloat16),
        sums + [routes.reshape(1, -1)],
    )

    def far(step):
        return lambda g, d: (g, d ^ (2 * step))

    grams, steps = [mine], [0]
    for step in sorted(range(1, z_size), key=lambda k: (-(k >= z_size // 2), k)):
        grams.append(move(mine, far(step * y_size)))
        steps.append(step * y_size)
    if y_size == 2:
        grams = grams + [move(x, to_y) for x in grams]
        steps = steps + [step ^ 1 for step in steps]
    columns = local(
        functools.partial(fisher_kernel, steps),
        "precondition",
        jax.ShapeDtypeStruct((EXPERTS, PROJ * PROJ), f32),
        grams + [move(x, to_core) for x in grams] + [fisher_inverse],
    )
    result = lax.all_to_all(columns, "dp", split_axis=1, concat_axis=1, tiled=True)
    return result.reshape(1, EXPERTS, PROJ * PROJ)


def solution(mesh):
    in_specs = (
        P(AXES, None),
        P(AXES, None),
        P(AXES, None),
        P(None, "dp"),
        P(None, "dp"),
        P(None, "dp"),
    )
    out_specs = P(AXES, None, None)
    return jax.shard_map(shards, mesh=mesh, in_specs=in_specs, out_specs=out_specs, check_vma=False)
```

```python
import functools

import jax
import jax.numpy as jnp
from jax import lax
from jax.experimental import pallas as pl
from jax.experimental.pallas import tpu as pltpu
from jax.sharding import PartitionSpec as P

EXPERTS = 8
PROJ = 64
TOK = 128
LANES = 128
VMEM = 28 * 1024 * 1024
AXES = ("groups", "dp")


def position():
    place = lax.axis_index("dp")
    return lax.rem(place, 2), lax.div(place, 2), lax.rem(lax.axis_index("groups"), 2)


def piece_of(at, sizes):
    z_size, y_size, slices = sizes
    _, chip, _ = position()
    z, y = lax.div(chip, y_size), lax.rem(chip, y_size)
    step, across = at
    first = 2 * (lax.rem(z + (step + z_size), z_size) * y_size + (1 - y if across else y))
    return lax.div(first, slices), lax.div(lax.rem(first, slices), 2)


def nt(rows, table):
    return lax.dot_general(rows, table, (((1,), (1,)), ((), ())), preferred_element_type=jnp.float32)


def pick(total, routes, experts, sub):
    low = lax.broadcasted_iota(jnp.int32, (TOK, LANES), 1) < PROJ
    out = []
    for k in range(2):
        picked = jnp.zeros((TOK, LANES), jnp.float32)
        for a in range(sub):
            for pair in range(len(experts) // 2):
                even, odd = experts[2 * pair], experts[2 * pair + 1]
                wanted = jnp.where(
                    low,
                    jnp.where(even[1] == a, even[0], -1),
                    jnp.where(odd[1] == a, odd[0], -1),
                ).astype(jnp.float32)
                picked += jnp.where(routes[:, k : k + 1] == wanted, total(a, pair), 0.0)
        out.append(picked + pltpu.roll(picked, PROJ, 1))
    return out


def right_sums(sub, width, toks, pieces):
    table = jnp.concatenate([p[:, :width] for p in pieces], axis=0)
    return [nt(toks[:, a * width : (a + 1) * width], table) for a in range(sub)]


def left_sums(sub, width, toks, pieces):
    table = jnp.concatenate([p[:, width:] for p in pieces], axis=0)
    at, size = sub * width, table.shape[1]
    return [nt(toks[:, at + a * size : at + (a + 1) * size], table) for a in range(sub)]


def picks(rows, tables, experts, width, sub):
    toks = jnp.concatenate(rows, axis=0)
    right, left = right_sums(sub, width, toks, tables), left_sums(sub, width, toks, tables)
    low = lax.broadcasted_iota(jnp.int32, (TOK, LANES), 1) < PROJ
    picked = []
    for b in range(len(rows)):
        here = slice(b * TOK, (b + 1) * TOK)
        named = toks[here, -LANES:].astype(jnp.float32)

        def pick_of(sums):
            return pick(lambda a, pair: sums[a][here, pair * LANES : (pair + 1) * LANES], named, experts, sub)

        picked.append([jnp.where(low, x, y) for x, y in zip(pick_of(left), pick_of(right))])
    return picked


def early_kernel(sub, width, ids, sizes, own, other, x, *refs):
    experts = [piece_of(at, sizes) for at in ids]
    rows = [own[...], other[...], x[...]]
    for b, slots in enumerate(picks(rows, refs[:-1], experts, width, sub)):
        for k, got in enumerate(slots):
            refs[-1][b, :, k * LANES : (k + 1) * LANES] = got


def late_kernel(sub, width, ids, sizes, own, other, x, early_ref, *refs):
    pieces, outs = refs[:-3], refs[-3:]
    experts = [piece_of(at, sizes) for at in ids]
    rows = [own[...], other[...], x[...]]
    for b, slots in enumerate(picks(rows, pieces, experts, width, sub)):
        for k, got in enumerate(slots):
            lanes = slice(k * LANES, (k + 1) * LANES)
            outs[b][:, lanes] = early_ref[b, :, lanes] + got


def last_kernel(sub, width, ids, sizes, xc, *refs):
    experts = [piece_of(at, sizes) for at in ids]
    for k, got in enumerate(picks([xc[...]], refs[:-1], experts, width, sub)[0]):
        refs[-1][:, k * LANES : (k + 1) * LANES] = got


def pack_kernel(outputs, routes_ref, *refs):
    core, _, half = position()
    n_blocks = sum(len(blocks) for blocks in outputs)
    ins, outs, routes, sems = refs[:n_blocks], refs[n_blocks:-2], refs[-2], refs[-1]
    copies, i = [], 0
    named = pltpu.make_async_copy(routes_ref, routes, sems.at[n_blocks])
    named.start()
    for blocks, out in zip(outputs, outs):
        at = 0
        for width, place, offset in blocks:
            start = pl.multiple_of((place(core, half) + offset) * width, LANES)
            copy = pltpu.make_async_copy(ins[i].at[:, pl.ds(start, width)], out.at[:, at : at + width], sems.at[i])
            copy.start()
            copies.append(copy)
            at, i = at + width, i + 1
    row = lax.broadcasted_iota(jnp.int32, (TOK, LANES), 0)
    named.wait()
    routes = routes[...].astype(jnp.float32)
    named = jnp.where(row == 0, routes[0:1], jnp.where(row == 1, routes[1:2], 0.0))
    named = jnp.transpose(named).astype(jnp.bfloat16)
    for blocks, out in zip(outputs, outs):
        size = sum(block[0] for block in blocks)
        if out.shape[1] > size:
            out[:, size:] = named
    for copy in copies:
        copy.wait()


def pack(routes, outputs, name):
    blocks = [b for out in outputs for b in out]
    shapes = []
    for out in outputs:
        rows = out[0][0].shape[0]
        shapes.append((rows, sum(b[1] for b in out) + (LANES if rows == TOK else 0)))
    return pl.pallas_call(
        functools.partial(pack_kernel, [[b[1:] for b in out] for out in outputs]),
        in_specs=[pl.BlockSpec(memory_space=pltpu.HBM)] * (1 + len(blocks)),
        out_specs=[pl.BlockSpec(memory_space=pltpu.VMEM)] * len(shapes),
        out_shape=[jax.ShapeDtypeStruct(x, jnp.bfloat16) for x in shapes],
        scratch_shapes=[pltpu.VMEM((2, TOK), jnp.int32), pltpu.SemaphoreType.DMA((len(blocks) + 1,))],
        compiler_params=pltpu.CompilerParams(vmem_limit_bytes=VMEM),
        name=name,
    )(*[pltpu.with_memory_space_constraint(x, pltpu.HBM) for x in [routes] + [b[0] for b in blocks]])


def local(kernel, name, out_shape, operands):
    vmem = pl.BlockSpec(memory_space=pltpu.VMEM)
    return pl.pallas_call(
        kernel,
        in_specs=[vmem] * len(operands),
        out_specs=jax.tree.map(lambda _: vmem, out_shape),
        out_shape=out_shape,
        compiler_params=pltpu.CompilerParams(vmem_limit_bytes=VMEM),
        name=name,
    )(*operands)


def gram_kernel(p0, p1, p2, p3, routes_ref, out_ref):
    total = (p0[...] + p1[...]) + (p2[...] + p3[...])
    first, second = total[:, :LANES], total[:, LANES:]
    left = jnp.concatenate([jnp.transpose(first)[:PROJ], jnp.transpose(second)[:PROJ]], axis=1)
    right = jnp.concatenate([first, second], axis=0)
    left_high, right_high = left.astype(jnp.bfloat16).astype(jnp.float32), right.astype(jnp.bfloat16)
    left_low, right_low = left - left_high, (right - right_high.astype(jnp.float32)).astype(jnp.bfloat16)
    expert = lax.broadcasted_iota(jnp.int32, (EXPERTS, 2 * TOK), 0)
    chosen = jnp.where(jnp.broadcast_to(routes_ref[...], expert.shape) == expert, 1.0, 0.0)

    def masked(x):
        rows = [x[p : p + 1] * chosen for p in range(PROJ)]
        return jnp.concatenate(rows, axis=0).astype(jnp.bfloat16)

    high, low = masked(left_high), masked(left_low)
    grams = jnp.dot(high, right_high, preferred_element_type=jnp.float32)
    grams += jnp.dot(high, right_low, preferred_element_type=jnp.float32)
    grams += jnp.dot(low, right_high, preferred_element_type=jnp.float32)
    grams = grams * (TOK**-0.5)
    rows = PROJ // 2 * EXPERTS
    first = lax.broadcasted_iota(jnp.int32, (rows, LANES), 1) < PROJ
    mine = jnp.where(first, pltpu.roll(grams[:rows], PROJ, 1), grams[rows:])
    out_ref[...] = mine.reshape(PROJ // 4, 2 * EXPERTS, LANES).astype(jnp.bfloat16)


def fisher_kernel(steps, *refs):
    n = len(steps)
    tables, out_ref = refs[n : n + 2], refs[n + 2]
    core, chip, _ = position()
    width = tables[0].shape[1]
    totals = [jnp.zeros((n * EXPERTS, width), jnp.float32) for _ in tables]
    for i in range(PROJ // 4):
        rows = jnp.concatenate([x[i].astype(jnp.float32).reshape(1, 2, EXPERTS, LANES) for x in refs[:n]], axis=0)
        for h in range(2):
            p = 2 * i + h
            lhs = rows[:, h].reshape(n * EXPERTS, LANES).astype(jnp.bfloat16)
            for k, fisher in enumerate(tables):
                table = jnp.concatenate(
                    [
                        fisher[p * PROJ : (p + 1) * PROJ, :],
                        fisher[(PROJ // 2 + p) * PROJ : (PROJ // 2 + p + 1) * PROJ, :],
                    ],
                    axis=0,
                )
                totals[k] += jnp.dot(lhs, table, preferred_element_type=jnp.float32)
    for j, step in enumerate(steps):
        for k, total in enumerate(totals):
            place = 2 * jnp.bitwise_xor(chip, step) + (1 - core if k else core)
            at = pl.multiple_of(place * width, LANES)
            out_ref[:, pl.ds(at, width)] = total[j * EXPERTS : (j + 1) * EXPERTS]


def shards(features, grads, routes, proj_in, proj_out, fisher_inverse):
    groups, n = lax.axis_size("groups"), lax.axis_size("dp")
    chips = n // 2
    slices = n // EXPERTS
    sub = slices // 2
    y_size = 2 if groups == 2 else 1
    z_size = chips // y_size
    def move(x, to):
        pairs = []
        for g in range(groups):
            for d in range(n):
                tg, td = to(g, d)
                pairs.append((g * n + d, tg * n + td))
        return lax.ppermute(x, AXES, pairs)

    def to_core(g, d):
        return g, d ^ 1

    def to_x(g, d):
        return g ^ 1, d

    def to_x_core(g, d):
        return g ^ 1, d ^ 1

    def to_y(g, d):
        return g, d ^ 2

    def to_z(g, d):
        return g, (d + 2 * y_size) % n

    def from_z(g, d):
        return g, (d - 2 * y_size) % n

    quarter_in, quarter_out = proj_in.shape[1] // 2, proj_out.shape[1] // 2

    def after(x, *others):
        return lax.optimization_barrier((x, *others))[0]

    def whole(place):
        return [(grads, quarter_out, place, 4 * a) for a in range(sub)] + [
            (features, quarter_in, place, 4 * a) for a in range(sub)
        ]

    def by_half(core, half):
        return half

    routes = routes.T
    table, send_other, send_x = pack(
        routes,
        [
            [(proj_out, quarter_out, by_half, 0), (proj_in, quarter_in, by_half, 0)],
            whole(lambda core, half: 2 * (1 - core) + half),
            whole(lambda core, half: 2 * core + 1 - half),
        ],
        "pack_first",
    )
    send_xc, own = pack(
        after(routes, send_x),
        [whole(lambda core, half: 2 * (1 - core) + 1 - half), whole(lambda core, half: 2 * core + half)],
        "pack_second",
    )

    facing = move(table, to_y) if y_size == 2 else table
    other, x = move(send_other, to_core), move(send_x, to_x)
    xc = move(after(send_xc, facing), to_x_core)
    blocks, ids = [table], [0]
    ups, downs = z_size // 2, (z_size - 1) // 2
    up = down = table
    for k in range(1, ups + 1):
        up = move(after(up, facing, other) if k == 2 else up, to_z)
        blocks.append(up)
        ids.append(-k)
        if k <= downs:
            down = move(down, from_z)
            blocks.append(down)
            ids.append(k)
    pieces, where = [], []
    for i, block in enumerate(blocks):
        for across in range(y_size):
            if across:
                if i == 1:
                    block = after(block, facing)
                block = facing if i == 0 else block
                if 0 < i < len(blocks) - 1:
                    block = move(block, to_y)
                if i == len(blocks) - 1:
                    near = move(after(block, x, pieces[3])[: PROJ // 2], to_y)
                    block = (near, move(pieces[3][PROJ // 2 :], to_z))
            pieces.append(block)
            where.append((ids[i] % z_size, across))

    f32 = jnp.float32
    sizes = (z_size, y_size, slices)
    early = local(
        functools.partial(early_kernel, sub, quarter_out, where[:-2], sizes),
        "project_early",
        jax.ShapeDtypeStruct((3, TOK, 2 * LANES), f32),
        [own, other, x] + pieces[:-2],
    )
    block = jax.ShapeDtypeStruct((TOK, 2 * LANES), f32)
    partial = local(
        functools.partial(late_kernel, sub, quarter_out, where[-2:], sizes),
        "project_late",
        [block] * 3,
        [own, other, x, early] + jax.tree.leaves(pieces[-2:]),
    )
    ending = local(
        functools.partial(last_kernel, sub, quarter_out, where, sizes),
        "project_last",
        block,
        [after(xc, partial[0])] + jax.tree.leaves(pieces),
    )
    sums = [partial[0], move(partial[1], to_core), move(partial[2], to_x), move(ending, to_x_core)]
    mine = local(
        gram_kernel,
        "gram",
        jax.ShapeDtypeStruct((PROJ // 4, 2 * EXPERTS, LANES), jnp.bfloat16),
        sums + [routes.reshape(1, -1)],
    )

    fisher_other = move(after(fisher_inverse, mine), to_core)
    def far(step):
        return lambda g, d: (g, d ^ (2 * step))

    grams, steps = [mine], [0]
    for step in sorted(range(1, z_size), key=lambda k: (-(k >= z_size // 2), k)):
        grams.append(move(mine, far(step * y_size)))
        steps.append(step * y_size)
    if y_size == 2:
        grams = grams + [move(x, to_y) for x in grams]
        steps = steps + [step ^ 1 for step in steps]
    columns = local(
        functools.partial(fisher_kernel, steps),
        "precondition",
        jax.ShapeDtypeStruct((EXPERTS, PROJ * PROJ), f32),
        grams + [fisher_inverse, fisher_other],
    )
    same_core = [list(range(c, n, 2)) for c in range(2)]
    result = lax.all_to_all(
        columns, "dp", split_axis=1, concat_axis=1, axis_index_groups=same_core, tiled=True
    )
    return result.reshape(1, EXPERTS, PROJ * PROJ)


def solution(mesh):
    in_specs = (
        P(AXES, None),
        P(AXES, None),
        P(AXES, None),
        P(None, "dp"),
        P(None, "dp"),
        P(None, "dp"),
    )
    out_specs = P(AXES, None, None)
    return jax.shard_map(shards, mesh=mesh, in_specs=in_specs, out_specs=out_specs, check_vma=False)
```

```python
import functools

import jax
import jax.numpy as jnp
from jax import lax
from jax.experimental import pallas as pl
from jax.experimental.pallas import tpu as pltpu
from jax.sharding import PartitionSpec as P

EXPERTS = 8
PROJ = 64
TOK = 128
LANES = 128
VMEM = 28 * 1024 * 1024
AXES = ("groups", "dp")


def position():
    place = lax.axis_index("dp")
    return lax.rem(place, 2), lax.div(place, 2), lax.rem(lax.axis_index("groups"), 2)


def piece_of(at, sizes):
    z_size, y_size, slices = sizes
    _, chip, _ = position()
    z, y = lax.div(chip, y_size), lax.rem(chip, y_size)
    step, across = at
    first = 2 * (lax.rem(z + (step + z_size), z_size) * y_size + (1 - y if across else y))
    return lax.div(first, slices), lax.div(lax.rem(first, slices), 2)


def nt(rows, table):
    return lax.dot_general(rows, table, (((1,), (1,)), ((), ())), preferred_element_type=jnp.float32)


def pick(total, routes, experts, sub):
    low = lax.broadcasted_iota(jnp.int32, (TOK, LANES), 1) < PROJ
    out = []
    for k in range(2):
        picked = jnp.zeros((TOK, LANES), jnp.float32)
        for a in range(sub):
            for pair in range(len(experts) // 2):
                even, odd = experts[2 * pair], experts[2 * pair + 1]
                wanted = jnp.where(
                    low,
                    jnp.where(even[1] == a, even[0], -1),
                    jnp.where(odd[1] == a, odd[0], -1),
                ).astype(jnp.float32)
                picked += jnp.where(routes[:, k : k + 1] == wanted, total(a, pair), 0.0)
        out.append(picked + pltpu.roll(picked, PROJ, 1))
    return out


def right_sums(sub, width, toks, pieces):
    table = jnp.concatenate([p[:, :width] for p in pieces], axis=0)
    return [nt(toks[:, a * width : (a + 1) * width], table) for a in range(sub)]


def left_sums(sub, width, toks, pieces):
    table = jnp.concatenate([p[:, width:] for p in pieces], axis=0)
    at, size = sub * width, table.shape[1]
    return [nt(toks[:, at + a * size : at + (a + 1) * size], table) for a in range(sub)]


def picks(rows, tables, experts, width, sub):
    toks = jnp.concatenate(rows, axis=0)
    right, left = right_sums(sub, width, toks, tables), left_sums(sub, width, toks, tables)
    low = lax.broadcasted_iota(jnp.int32, (TOK, LANES), 1) < PROJ
    picked = []
    for b in range(len(rows)):
        here = slice(b * TOK, (b + 1) * TOK)
        named = toks[here, -LANES:].astype(jnp.float32)

        def pick_of(sums):
            return pick(lambda a, pair: sums[a][here, pair * LANES : (pair + 1) * LANES], named, experts, sub)

        picked.append([jnp.where(low, x, y) for x, y in zip(pick_of(left), pick_of(right))])
    return picked


def early_kernel(sub, width, ids, sizes, own, other, x, *refs):
    experts = [piece_of(at, sizes) for at in ids]
    rows = [own[...], other[...], x[...]]
    for b, slots in enumerate(picks(rows, refs[:-1], experts, width, sub)):
        for k, got in enumerate(slots):
            refs[-1][b, :, k * LANES : (k + 1) * LANES] = got


def late_kernel(sub, width, ids, sizes, own, other, x, early_ref, *refs):
    pieces, outs = refs[:-3], refs[-3:]
    experts = [piece_of(at, sizes) for at in ids]
    rows = [own[...], other[...], x[...]]
    for b, slots in enumerate(picks(rows, pieces, experts, width, sub)):
        for k, got in enumerate(slots):
            lanes = slice(k * LANES, (k + 1) * LANES)
            outs[b][:, lanes] = early_ref[b, :, lanes] + got


def last_kernel(sub, width, ids, sizes, xc, *refs):
    pieces, out = refs[:-1], refs[-1]
    toks = xc[...]
    named = jnp.transpose(toks[:, -LANES:].astype(jnp.float32))
    sides = []
    for at, size, table in (
        (sub * width, pieces[0].shape[1] - width, jnp.concatenate([p[:, width:] for p in pieces], axis=0)),
        (0, width, jnp.concatenate([p[:, :width] for p in pieces], axis=0)),
    ):
        sides.append([nt(table, toks[:, at + a * size : at + (a + 1) * size]) for a in range(sub)])
    for k in range(2):
        parts = []
        for sums in sides:
            picked = jnp.zeros((PROJ, TOK), jnp.float32)
            for i, place in enumerate(ids):
                expert, part = piece_of(place, sizes)
                for a in range(sub):
                    wanted = jnp.where(part == a, expert, -1).astype(jnp.float32)
                    picked += jnp.where(named[k : k + 1] == wanted, sums[a][i * PROJ : (i + 1) * PROJ], 0.0)
            parts.append(picked)
        out[:, k * LANES : (k + 1) * LANES] = jnp.transpose(jnp.concatenate(parts, axis=0))


def pack_kernel(outputs, routes_ref, *refs):
    core, _, half = position()
    n_blocks = sum(len(blocks) for blocks in outputs)
    ins, outs, routes, sems = refs[:n_blocks], refs[n_blocks:-2], refs[-2], refs[-1]
    copies, i = [], 0
    named = pltpu.make_async_copy(routes_ref, routes, sems.at[n_blocks])
    named.start()
    for blocks, out in zip(outputs, outs):
        at = 0
        for width, place, offset in blocks:
            start = pl.multiple_of((place(core, half) + offset) * width, LANES)
            copy = pltpu.make_async_copy(ins[i].at[:, pl.ds(start, width)], out.at[:, at : at + width], sems.at[i])
            copy.start()
            copies.append(copy)
            at, i = at + width, i + 1
    row = lax.broadcasted_iota(jnp.int32, (TOK, LANES), 0)
    named.wait()
    routes = routes[...].astype(jnp.float32)
    named = jnp.where(row == 0, routes[0:1], jnp.where(row == 1, routes[1:2], 0.0))
    named = jnp.transpose(named).astype(jnp.bfloat16)
    for blocks, out in zip(outputs, outs):
        size = sum(block[0] for block in blocks)
        if out.shape[1] > size:
            out[:, size:] = named
    for copy in copies:
        copy.wait()


def pack(routes, outputs, name):
    blocks = [b for out in outputs for b in out]
    shapes = []
    for out in outputs:
        rows = out[0][0].shape[0]
        shapes.append((rows, sum(b[1] for b in out) + (LANES if rows == TOK else 0)))
    return pl.pallas_call(
        functools.partial(pack_kernel, [[b[1:] for b in out] for out in outputs]),
        in_specs=[pl.BlockSpec(memory_space=pltpu.HBM)] * (1 + len(blocks)),
        out_specs=[pl.BlockSpec(memory_space=pltpu.VMEM)] * len(shapes),
        out_shape=[jax.ShapeDtypeStruct(x, jnp.bfloat16) for x in shapes],
        scratch_shapes=[pltpu.VMEM((2, TOK), jnp.int32), pltpu.SemaphoreType.DMA((len(blocks) + 1,))],
        compiler_params=pltpu.CompilerParams(vmem_limit_bytes=VMEM),
        name=name,
    )(*[pltpu.with_memory_space_constraint(x, pltpu.HBM) for x in [routes] + [b[0] for b in blocks]])


def local(kernel, name, out_shape, operands):
    vmem = pl.BlockSpec(memory_space=pltpu.VMEM)
    return pl.pallas_call(
        kernel,
        in_specs=[vmem] * len(operands),
        out_specs=jax.tree.map(lambda _: vmem, out_shape),
        out_shape=out_shape,
        compiler_params=pltpu.CompilerParams(vmem_limit_bytes=VMEM),
        name=name,
    )(*operands)


def gram_kernel(p0, p1, p2, p3, routes_ref, out_ref):
    total = (p0[...] + p1[...]) + (p2[...] + p3[...])
    first, second = total[:, :LANES], total[:, LANES:]
    left = jnp.concatenate([jnp.transpose(first)[:PROJ], jnp.transpose(second)[:PROJ]], axis=1)
    right = jnp.concatenate([first, second], axis=0)
    left_high, right_high = left.astype(jnp.bfloat16).astype(jnp.float32), right.astype(jnp.bfloat16)
    left_low, right_low = left - left_high, (right - right_high.astype(jnp.float32)).astype(jnp.bfloat16)
    expert = lax.broadcasted_iota(jnp.int32, (EXPERTS, 2 * TOK), 0)
    chosen = jnp.where(jnp.broadcast_to(routes_ref[...], expert.shape) == expert, 1.0, 0.0)

    def masked(x):
        rows = [x[p : p + 1] * chosen for p in range(PROJ)]
        return jnp.concatenate(rows, axis=0).astype(jnp.bfloat16)

    high, low = masked(left_high), masked(left_low)
    grams = jnp.dot(high, right_high, preferred_element_type=jnp.float32)
    grams += jnp.dot(high, right_low, preferred_element_type=jnp.float32)
    grams += jnp.dot(low, right_high, preferred_element_type=jnp.float32)
    grams = grams * (TOK**-0.5)
    rows = PROJ // 2 * EXPERTS
    first = lax.broadcasted_iota(jnp.int32, (rows, LANES), 1) < PROJ
    mine = jnp.where(first, pltpu.roll(grams[:rows], PROJ, 1), grams[rows:])
    out_ref[...] = mine.reshape(PROJ // 4, 2 * EXPERTS, LANES).astype(jnp.bfloat16)


def fisher_kernel(steps, *refs):
    n = len(steps)
    tables, out_ref = refs[n : n + 2], refs[n + 2]
    core, chip, _ = position()
    width = tables[0].shape[1]
    totals = [jnp.zeros((n * EXPERTS, width), jnp.float32) for _ in tables]
    for i in range(PROJ // 4):
        rows = jnp.concatenate([x[i].astype(jnp.float32).reshape(1, 2, EXPERTS, LANES) for x in refs[:n]], axis=0)
        for h in range(2):
            p = 2 * i + h
            lhs = rows[:, h].reshape(n * EXPERTS, LANES).astype(jnp.bfloat16)
            for k, fisher in enumerate(tables):
                table = jnp.concatenate(
                    [
                        fisher[p * PROJ : (p + 1) * PROJ, :],
                        fisher[(PROJ // 2 + p) * PROJ : (PROJ // 2 + p + 1) * PROJ, :],
                    ],
                    axis=0,
                )
                totals[k] += jnp.dot(lhs, table, preferred_element_type=jnp.float32)
    for j, step in enumerate(steps):
        for k, total in enumerate(totals):
            place = 2 * jnp.bitwise_xor(chip, step) + (1 - core if k else core)
            at = pl.multiple_of(place * width, LANES)
            out_ref[:, pl.ds(at, width)] = total[j * EXPERTS : (j + 1) * EXPERTS]


def shards(features, grads, routes, proj_in, proj_out, fisher_inverse):
    groups, n = lax.axis_size("groups"), lax.axis_size("dp")
    chips = n // 2
    slices = n // EXPERTS
    sub = slices // 2
    y_size = 2 if groups == 2 else 1
    z_size = chips // y_size
    def move(x, to):
        pairs = []
        for g in range(groups):
            for d in range(n):
                tg, td = to(g, d)
                pairs.append((g * n + d, tg * n + td))
        return lax.ppermute(x, AXES, pairs)

    def to_core(g, d):
        return g, d ^ 1

    def to_x(g, d):
        return g ^ 1, d

    def to_x_core(g, d):
        return g ^ 1, d ^ 1

    def to_y(g, d):
        return g, d ^ 2

    def to_z(g, d):
        return g, (d + 2 * y_size) % n

    def from_z(g, d):
        return g, (d - 2 * y_size) % n

    quarter_in, quarter_out = proj_in.shape[1] // 2, proj_out.shape[1] // 2

    def after(x, *others):
        return lax.optimization_barrier((x, *others))[0]

    def whole(place):
        return [(grads, quarter_out, place, 4 * a) for a in range(sub)] + [
            (features, quarter_in, place, 4 * a) for a in range(sub)
        ]

    def by_half(core, half):
        return half

    routes = routes.T
    table, send_other, send_x = pack(
        routes,
        [
            [(proj_out, quarter_out, by_half, 0), (proj_in, quarter_in, by_half, 0)],
            whole(lambda core, half: 2 * (1 - core) + half),
            whole(lambda core, half: 2 * core + 1 - half),
        ],
        "pack_first",
    )
    send_xc, own = pack(
        after(routes, send_x),
        [whole(lambda core, half: 2 * (1 - core) + 1 - half), whole(lambda core, half: 2 * core + half)],
        "pack_second",
    )

    facing = move(table, to_y) if y_size == 2 else table
    other, x = move(send_other, to_core), move(send_x, to_x)
    xc = move(after(send_xc, facing), to_x_core)
    blocks, ids = [table], [0]
    ups, downs = z_size // 2, (z_size - 1) // 2
    up = down = table
    for k in range(1, ups + 1):
        up = move(after(up, facing, other) if k == 2 else up, to_z)
        blocks.append(up)
        ids.append(-k)
        if k <= downs:
            down = move(down, from_z)
            blocks.append(down)
            ids.append(k)
    pieces, where = [], []
    for i, block in enumerate(blocks):
        for across in range(y_size):
            if across:
                if i == 1:
                    block = after(block, facing)
                block = facing if i == 0 else block
                if 0 < i < len(blocks) - 1:
                    block = move(block, to_y)
                if i == len(blocks) - 1:
                    near = move(after(block, x, pieces[3])[: PROJ // 2], to_y)
                    block = (near, move(pieces[3][PROJ // 2 :], to_z))
            pieces.append(block)
            where.append((ids[i] % z_size, across))

    f32 = jnp.float32
    sizes = (z_size, y_size, slices)
    early = local(
        functools.partial(early_kernel, sub, quarter_out, where[:-2], sizes),
        "project_early",
        jax.ShapeDtypeStruct((3, TOK, 2 * LANES), f32),
        [own, other, x] + pieces[:-2],
    )
    block = jax.ShapeDtypeStruct((TOK, 2 * LANES), f32)
    partial = local(
        functools.partial(late_kernel, sub, quarter_out, where[-2:], sizes),
        "project_late",
        [block] * 3,
        [own, other, x, early] + jax.tree.leaves(pieces[-2:]),
    )
    ending = local(
        functools.partial(last_kernel, sub, quarter_out, where, sizes),
        "project_last",
        block,
        [after(xc, partial[0])] + jax.tree.leaves(pieces),
    )
    sums = [partial[0], move(partial[1], to_core), move(partial[2], to_x), move(ending, to_x_core)]
    mine = local(
        gram_kernel,
        "gram",
        jax.ShapeDtypeStruct((PROJ // 4, 2 * EXPERTS, LANES), jnp.bfloat16),
        sums + [routes.reshape(1, -1)],
    )

    fisher_other = move(after(fisher_inverse, mine), to_core)
    def far(step):
        return lambda g, d: (g, d ^ (2 * step))

    grams, steps = [mine], [0]
    for step in range(1, z_size):
        grams.append(move(mine, far(step * y_size)))
        steps.append(step * y_size)
    if y_size == 2:
        grams = grams + [move(x, to_y) for x in grams]
        steps = steps + [step ^ 1 for step in steps]
    columns = local(
        functools.partial(fisher_kernel, steps),
        "precondition",
        jax.ShapeDtypeStruct((EXPERTS, PROJ * PROJ), f32),
        grams + [fisher_inverse, fisher_other],
    )
    same_core = [list(range(c, n, 2)) for c in range(2)]
    result = lax.all_to_all(
        columns, "dp", split_axis=1, concat_axis=1, axis_index_groups=same_core, tiled=True
    )
    return result.reshape(1, EXPERTS, PROJ * PROJ)


def solution(mesh):
    in_specs = (
        P(AXES, None),
        P(AXES, None),
        P(AXES, None),
        P(None, "dp"),
        P(None, "dp"),
        P(None, "dp"),
    )
    out_specs = P(AXES, None, None)
    return jax.shard_map(shards, mesh=mesh, in_specs=in_specs, out_specs=out_specs, check_vma=False)
```
